256 devices in a mesh: clip: 8 (over y, core), seq: 16 (over z, x_lo), tp: 2 (over x_hi).
Axes of the slice: x: 4 (x_hi: 2, x_lo: 2; x = x_hi * 2 + x_lo), y: 4, z: 8, core: 2. Of those that a mesh axis runs over, the one named last changes fastest.
Arguments:
- frames: bfloat16 [768, 128, 1152], P('tp', ('clip', 'seq')), parts along dimension 1, may hold values from -6 to 6
- timestep: int32 [8], P('clip'), parts along dimension 0, may hold values from 0 to 999
- embed_weight: bfloat16 [256, 1152], replicated, may hold values from -0.375 to 0.375
- block_weight: bfloat16 [1152, 3456], P(('seq', 'tp')), may hold values from -0.1875 to 0.1875
- spatial_table: float32 [3, 1152], replicated, may hold values from -3 to 3
- temporal_table: float32 [3, 1152], replicated, may hold values from -3 to 3
- spatial_qkv: bfloat16 [1152, 3, 1152], P(None, None, 'tp'), may hold values from -1 to 1
- spatial_out: bfloat16 [1152, 1152], P('tp'), may hold values from -0.1875 to 0.1875
- temporal_qkv: bfloat16 [1152, 3, 1152], P(None, None, 'tp'), may hold values from -1 to 1
- temporal_out: bfloat16 [1152, 1152], P('tp'), may hold values from -0.1875 to 0.1875
Outputs:
- mixed: float32 [768, 128, 1152], P('tp', ('clip', 'seq')), parts along dimension 1
The draws below stay inside these ranges and needn't reach their ends.
There are 8 independent parts, one for each index of `clip`. The reference program is written for one: setup_inputs(seed, part) draws one part's arguments, and reference() takes and returns one part's arrays. A program takes and returns all parts, laid end to end along the dimension named above; an argument that names none is the same for every part. Nothing has to cross between parts.
All inputs are finite; a program needn't handle non-finite values.
Results may differ from the reference program's by a relative error of at most 0.0085.
Values may be sent and summed in bfloat16 or wider, within the bound.
No kernel may reach another device: no remote copies, remote signals or barrier semaphores. Data moves between devices by JAX's collectives and lax.ppermute only.
A program may use at most 128 MiB of HBM per device.

```python
import math
import jax
import jax.numpy as jnp
from jax import lax

D = 1152
HEADS = 16
HEAD_DIM = 72
FREQ = 256
SPATIAL = 768
FRAMES = 16


def draw_spatial_qkv(key, part):
    key = jax.random.fold_in(key, 11)
    return jnp.clip(jax.random.normal(key, (D, 3, D), jnp.float32) / math.sqrt(D), -1.0, 1.0).astype(jnp.bfloat16)


def draw_temporal_qkv(key, part):
    key = jax.random.fold_in(key, 12)
    return jnp.clip(jax.random.normal(key, (D, 3, D), jnp.float32) / math.sqrt(D), -1.0, 1.0).astype(jnp.bfloat16)


def block_scale(own_key, extent, shards, least, high):
    loudness = 1.0
    for position, shards_of in shards:
        draws = jax.random.uniform(jax.random.fold_in(jax.random.fold_in(own_key, 6), position), (shards_of,), jnp.float32, least / len(shards), high / len(shards))
        loudness = loudness * jnp.repeat(jnp.exp(draws), extent[position] // shards_of).reshape((-1,) + (1,) * (len(extent) - 1 - position))
    return loudness


def gaussian(key, extent, deviation, limit, shards=(), kind=jnp.bfloat16):
    level = block_scale(key, extent, shards, -0.22, 0.18) if shards else 1.0
    values = jax.random.normal(key, extent, jnp.float32) * deviation * level
    return jnp.minimum(jnp.maximum(values, -limit), limit).astype(kind)


def setup_inputs(seed: int = 0, part: int = 0) -> dict:
    arg_keys = jax.random.split(jax.random.key(seed), 11)
    part_splits = jax.random.split(jax.random.fold_in(arg_keys[10], part), 11)
    return {
        "frames": gaussian(part_splits[0], (SPATIAL, FRAMES, D), 1.0, 6.0, ((0, 2), (1, 16))),
        "timestep": jax.random.randint(part_splits[1], (1,), 0, 1000).astype(jnp.int32),
        "embed_weight": gaussian(arg_keys[2], (FREQ, D), FREQ ** -0.5, 0.375),
        "block_weight": gaussian(arg_keys[3], (D, 3 * D), D ** -0.5, 0.1875, ((0, 32),)),
        "spatial_table": gaussian(arg_keys[4], (3, D), 0.5, 3.0, (), jnp.float32),
        "temporal_table": gaussian(arg_keys[5], (3, D), 0.5, 3.0, (), jnp.float32),
        "spatial_qkv": draw_spatial_qkv(jax.random.fold_in(arg_keys[10], 71), part),
        "spatial_out": gaussian(arg_keys[7], (D, D), D ** -0.5, 0.1875, ((0, 2),)),
        "temporal_qkv": draw_temporal_qkv(jax.random.fold_in(arg_keys[10], 71), part),
        "temporal_out": gaussian(arg_keys[9], (D, D), D ** -0.5, 0.1875, ((0, 2),)),
    }


def layer_norm(values):
    mean = lax.optimization_barrier(jnp.mean(values, axis=-1, keepdims=True))
    centred = values - mean
    variance = lax.optimization_barrier(jnp.mean(centred * centred, axis=-1, keepdims=True))
    return centred * lax.rsqrt(variance + 1e-06)

def modulate(tokens, mods):
    normed = layer_norm(tokens.astype(jnp.float32))
    return (normed * (1.0 + mods[1]) + mods[0]).astype(jnp.bfloat16)

def residual_add(tokens, mods, projected):
    return tokens.astype(jnp.float32) + mods[2] * projected

def soft_weights(scores):
    peak = lax.optimization_barrier(jnp.max(scores, axis=-1, keepdims=True))
    raised = jnp.exp(scores - peak)
    return (raised / lax.optimization_barrier(jnp.sum(raised, axis=-1, keepdims=True))).astype(jnp.bfloat16)

def time_features(timestep):
    half = FREQ // 2
    ladder = jnp.exp(-math.log(10000.0) * jnp.arange(half, dtype=jnp.float32) / half)
    angles = timestep.astype(jnp.float32)[:, None] * ladder[None, :]
    return jnp.concatenate([jnp.cos(angles), jnp.sin(angles)], axis=-1)

def project(attended, out_weight):
    return jnp.dot(attended, out_weight, preferred_element_type=jnp.float32)

def reference(frames, timestep, embed_weight, block_weight, spatial_table, temporal_table, spatial_qkv, spatial_out, temporal_qkv, temporal_out):
    features = time_features(timestep)
    embedded = jax.nn.silu(jnp.dot(features, embed_weight.astype(jnp.float32), precision=lax.Precision.HIGHEST))
    modulation = jnp.dot(embedded, block_weight.astype(jnp.float32), precision=lax.Precision.HIGHEST).reshape(3, D)
    spatial_mods = spatial_table + modulation
    temporal_mods = temporal_table + modulation
    factor = 1.0 / math.sqrt(HEAD_DIM)

    def one_frame(tokens):
        normed = modulate(tokens, spatial_mods)
        qkv = jnp.dot(normed, spatial_qkv.reshape(D, 3 * D), preferred_element_type=jnp.float32).astype(jnp.bfloat16)
        grid = qkv.reshape(SPATIAL, 3, HEADS, HEAD_DIM).astype(jnp.float32)
        scores = jnp.einsum('qhd,khd->hqk', grid[:, 0], grid[:, 1]) * factor
        weights = soft_weights(scores)
        attended = jnp.einsum('hqk,khd->qhd', weights.astype(jnp.float32), grid[:, 2])
        attended = attended.astype(jnp.bfloat16).reshape(SPATIAL, D)
        return residual_add(tokens, spatial_mods, project(attended, spatial_out))
    by_frame = jnp.swapaxes(frames, 0, 1)
    middle = jnp.swapaxes(lax.map(one_frame, by_frame), 0, 1)
    normed = modulate(middle, temporal_mods)
    qkv = jnp.dot(normed, temporal_qkv.reshape(D, 3 * D), preferred_element_type=jnp.float32).astype(jnp.bfloat16)
    grid = qkv.reshape(SPATIAL, FRAMES, 3, HEADS, HEAD_DIM).astype(jnp.float32)
    scores = jnp.einsum('pfhd,pghd->phfg', grid[:, :, 0], grid[:, :, 1]) * factor
    weights = soft_weights(scores)
    attended = jnp.einsum('phfg,pghd->pfhd', weights.astype(jnp.float32), grid[:, :, 2])
    attended = attended.astype(jnp.bfloat16).reshape(SPATIAL, FRAMES, D)
    return residual_add(middle, temporal_mods, project(attended, temporal_out))
```

```python
import math

import jax
import jax.numpy as jnp
from jax import lax
from jax.sharding import PartitionSpec as P

HEAD_DIM = 72
FREQ = 256
SWAP = [(0, 1), (1, 0)]


def layer_norm(values):
    mean = jnp.mean(values, axis=-1, keepdims=True)
    centred = values - mean
    variance = jnp.mean(centred * centred, axis=-1, keepdims=True)
    return centred * lax.rsqrt(variance + 1e-06)


def modulate(tokens, mods):
    normed = layer_norm(tokens.astype(jnp.float32))
    return (normed * (1.0 + mods[1]) + mods[0]).astype(jnp.bfloat16)


def time_features(timestep):
    half = FREQ // 2
    ladder = jnp.exp(-math.log(10000.0) * jnp.arange(half, dtype=jnp.float32) / half)
    angles = timestep.astype(jnp.float32)[:, None] * ladder[None, :]
    return jnp.concatenate([jnp.cos(angles), jnp.sin(angles)], axis=-1)


def modulation_rows(timestep, embed_weight, block_weight):
    features = time_features(timestep)
    embedded = jax.nn.silu(
        jnp.dot(features, embed_weight.astype(jnp.float32), precision=lax.Precision.HIGHEST)
    )
    count, width = block_weight.shape
    group = lax.axis_size("seq") * lax.axis_size("tp")
    start = lax.axis_index(("seq", "tp")) * count
    mine = lax.dynamic_slice_in_dim(embedded, start, count, 1)
    term = jnp.dot(mine, block_weight.astype(jnp.float32), precision=lax.Precision.HIGHEST)
    rows = 32
    term = jnp.pad(term.reshape(width // 128, 128), ((0, rows - width // 128), (0, 0)))
    copies = jnp.broadcast_to(term[None], (group, rows, 128)).reshape(group * rows, 128)
    terms = lax.all_to_all(copies, ("seq", "tp"), 0, 0, tiled=True)
    total = jnp.sum(terms.reshape(group, rows, 128), axis=0)
    return total.reshape(-1)[:width].reshape(3, -1)


def other_half(weight):
    eighth = weight.shape[0] // lax.axis_size("clip")
    piece = lax.dynamic_slice_in_dim(weight, lax.axis_index("clip") * eighth, eighth, 0)
    group = lax.axis_size("seq") * lax.axis_size("tp")
    piece = lax.ppermute(piece, ("seq", "tp"), [(i, i ^ 3) for i in range(group)])
    return lax.all_gather(piece, "clip", axis=0, tiled=True)


def attend(scores, values, out):
    peak = jnp.max(scores, axis=-1, keepdims=True)
    raised = jnp.exp(scores - peak)
    weights = (raised / jnp.sum(raised, axis=-1, keepdims=True)).astype(jnp.bfloat16)
    return jnp.einsum(out, weights, values, preferred_element_type=jnp.float32)


def project_in(tokens, weight):
    return lax.dot_general(
        tokens, weight, (((1,), (1,)), ((), ())), preferred_element_type=jnp.float32
    ).astype(jnp.bfloat16)


def spatial_attend(queries, keys, values):
    scores = jnp.einsum("qhd,khd->hqk", queries, keys, preferred_element_type=jnp.float32)
    out = attend(scores / math.sqrt(HEAD_DIM), values, "hqk,khd->qhd")
    return out.astype(jnp.bfloat16).reshape(queries.shape[0], -1)


def temporal_attend(qkv, depth):
    grid = qkv.reshape(depth, -1, 3, 8, HEAD_DIM)
    scores = jnp.einsum(
        "fphd,gphd->phfg", grid[:, :, 0], grid[:, :, 1], preferred_element_type=jnp.float32
    )
    out = attend(scores / math.sqrt(HEAD_DIM), grid[:, :, 2], "phfg,gphd->fphd")
    return out.astype(jnp.bfloat16).reshape(qkv.shape[0], -1)


def body(
    frames,
    timestep,
    embed_weight,
    block_weight,
    spatial_table,
    temporal_table,
    spatial_qkv,
    spatial_out,
    temporal_qkv,
    temporal_out,
):
    width = frames.shape[-1]
    tokens = frames.reshape(-1, width)
    count = tokens.shape[0]
    partner = lax.ppermute(tokens, "tp", SWAP)
    spatial_in = jnp.transpose(spatial_qkv, (1, 2, 0)).reshape(-1, width)
    temporal_in = jnp.transpose(temporal_qkv, (1, 2, 0)).reshape(-1, width)
    spatial_out_other = other_half(spatial_out)
    temporal_in_other = other_half(temporal_in)
    temporal_out_other = other_half(temporal_out)

    modulation = modulation_rows(timestep, embed_weight, block_weight)
    spatial_mods = spatial_table + modulation
    temporal_mods = temporal_table + modulation

    own = project_in(modulate(tokens, spatial_mods), spatial_in)
    far = project_in(modulate(partner, spatial_mods), spatial_in)
    grid = jnp.concatenate([own, far], axis=0).reshape(2 * count, 3, 8, HEAD_DIM)
    attended_far = spatial_attend(grid[count:, 0], grid[:, 1], grid[:, 2])
    attended_other = lax.ppermute(attended_far, "tp", SWAP)
    attended_own = spatial_attend(grid[:count, 0], grid[:, 1], grid[:, 2])
    projected = jnp.dot(attended_own, spatial_out, preferred_element_type=jnp.float32)
    projected += jnp.dot(attended_other, spatial_out_other, preferred_element_type=jnp.float32)
    middle = tokens.astype(jnp.float32) + spatial_mods[2] * projected

    normed = modulate(middle, temporal_mods)
    moved = lax.all_to_all(normed, "seq", 0, 0, tiled=True)
    depth = lax.axis_size("seq")
    attended = jnp.concatenate(
        [
            temporal_attend(project_in(moved, temporal_in), depth),
            temporal_attend(project_in(moved, temporal_in_other), depth),
        ],
        axis=1,
    )
    returned = lax.all_to_all(attended, "seq", 0, 0, tiled=True)
    half = temporal_out.shape[0]
    projected = jnp.dot(returned[:, :half], temporal_out, preferred_element_type=jnp.float32)
    projected += jnp.dot(
        returned[:, half:], temporal_out_other, preferred_element_type=jnp.float32
    )
    return (middle + temporal_mods[2] * projected).reshape(frames.shape)


def solution(mesh):
    return jax.shard_map(
        body,
        mesh=mesh,
        in_specs=(
            P("tp", ("clip", "seq"), None),
            P("clip"),
            P(),
            P(("seq", "tp"), None),
            P(),
            P(),
            P(None, None, "tp"),
            P("tp", None),
            P(None, None, "tp"),
            P("tp", None),
        ),
        out_specs=P("tp", ("clip", "seq"), None),
        check_vma=False,
    )
```

```python
import functools
import math

import jax
import jax.numpy as jnp
from jax import lax
from jax.experimental import pallas as pl
from jax.experimental.pallas import tpu as pltpu
from jax.sharding import PartitionSpec as P

HEAD_DIM = 72
FREQ = 256
LANES = 128
SWAP = [(0, 1), (1, 0)]
VMEM = pl.BlockSpec(memory_space=pltpu.VMEM)
SMEM = pl.BlockSpec(memory_space=pltpu.SMEM)
HBM = pl.BlockSpec(memory_space=pl.ANY)
TERM_ROWS = 32
CHUNKS = 2
SCALE = math.log2(math.e) / math.sqrt(HEAD_DIM)
BF16 = jnp.bfloat16
F32 = jnp.float32


def call(kernel, outs, in_specs, scratch=(), flops=0, nbytes=0, out_specs=None, mib=60):
    return pl.pallas_call(
        kernel,
        out_shape=outs,
        in_specs=in_specs,
        out_specs=out_specs or jax.tree.map(lambda _: VMEM, outs),
        scratch_shapes=list(scratch),
        compiler_params=pltpu.CompilerParams(vmem_limit_bytes=mib * 1024 * 1024),
        cost_estimate=pl.CostEstimate(flops=flops, bytes_accessed=nbytes, transcendentals=0),
    )


def dot_nt(a, b):
    return lax.dot_general(a, b, (((1,), (1,)), ((), ())), preferred_element_type=F32)


def normalise(tokens, shift, scale):
    mean = jnp.mean(tokens, axis=-1, keepdims=True)
    centred = tokens - mean
    variance = jnp.mean(centred * centred, axis=-1, keepdims=True)
    return (centred * lax.rsqrt(variance + 1e-06) * (1.0 + scale) + shift).astype(BF16)


def fetch(source, target, sem):
    copy = pltpu.make_async_copy(source, target, sem)
    copy.start()
    return copy


def window(head):
    first = head * HEAD_DIM // LANES * LANES
    last = -(-(head + 1) * HEAD_DIM // LANES) * LANES
    return first, last


def padded(width):
    return -(-width // LANES) * LANES


def head_queries(queries, head):
    first, last = window(head)
    start = head * HEAD_DIM
    pieces = [queries[start : start + HEAD_DIM]]
    tokens = queries.shape[1]
    if start > first:
        pieces.insert(0, jnp.zeros((start - first, tokens), F32))
    if last > start + HEAD_DIM:
        pieces.append(jnp.zeros((last - start - HEAD_DIM, tokens), F32))
    return jnp.concatenate(pieces, axis=0).astype(BF16)


def head_values(values, head):
    start = head * HEAD_DIM
    ones = jnp.ones((8, values.shape[1]), F32)
    return jnp.concatenate([values[start : start + HEAD_DIM], ones], axis=0).astype(BF16)


def head_scores(queries, keys, head):
    first, last = window(head)
    return jnp.dot(keys[:, first:last], head_queries(queries, head), preferred_element_type=F32)


def head_output(scores, values):
    peak = jnp.max(scores, axis=0, keepdims=True)
    raised = jnp.exp2(scores - peak).astype(BF16)
    out = jnp.dot(values, raised, preferred_element_type=F32)
    return out[:HEAD_DIM] / out[HEAD_DIM : HEAD_DIM + 1]


def modulation_table(terms, table):
    group = terms.shape[0] // TERM_ROWS
    total = jnp.sum(terms[...].reshape(group, TERM_ROWS, LANES), axis=0)
    tiles = table.shape[1] // LANES
    rows = []
    for row in range(3):
        parts = [total[row * tiles + t : row * tiles + t + 1] for t in range(tiles)]
        rows.append(jnp.concatenate(parts, axis=1))
    return jnp.concatenate(rows, axis=0)


def fetch_parts(w_hbm, w, sems):
    half = w.shape[1]
    return [fetch(w_hbm.at[pl.ds(p * half, half)], w.at[p], sems.at[p]) for p in range(3)]


def spatial_kernel(
    heads,
    tok_hbm,
    far_hbm,
    terms_hbm,
    table,
    next_table,
    w_hbm,
    after,
    mods_out,
    next_out,
    q_out,
    k_out,
    v_out,
    att_out,
    tok,
    far,
    terms,
    w,
    q,
    near_q,
    k,
    v,
    scores,
    sems,
):
    count, half = far.shape[0], heads * HEAD_DIM
    in_terms = fetch(terms_hbm, terms, sems.at[3])
    in_far = fetch(far_hbm, far, sems.at[4])
    in_w = fetch_parts(w_hbm, w, sems)
    in_tok = fetch(tok_hbm, tok, sems.at[5])
    near, beyond = pl.ds(0, count), pl.ds(count, count)
    k[:, k.shape[1] - LANES :] = jnp.zeros((2 * count, LANES), BF16)
    in_terms.wait()
    modulation = modulation_table(terms, table)
    mods = table[...] + modulation
    mods_out[...] = mods
    next_out[...] = next_table[...] + modulation
    in_far.wait()
    normed_far = normalise(far[...].astype(F32), mods[0:1], mods[1:2])
    in_w[0].wait()
    q[...] = dot_nt(w[0], normed_far) * SCALE
    in_w[1].wait()
    k[beyond, :half] = dot_nt(normed_far, w[1]).astype(BF16)
    in_tok.wait()
    normed = normalise(tok[...].astype(F32), mods[0:1], mods[1:2])
    k[near, :half] = dot_nt(normed, w[1]).astype(BF16)
    out_k = fetch(k, k_out, sems.at[6])
    for head in range(heads):
        scores[head] = head_scores(q, k, head)
    in_w[2].wait()
    values = dot_nt(w[2], normed)
    for head in range(heads):
        v[head, :, :count] = head_values(values, head)
    values = dot_nt(w[2], normed_far)
    for head in range(heads):
        v[head, :, count:] = head_values(values, head)
    out_v = fetch(v, v_out, sems.at[7])
    near_q[...] = (dot_nt(w[0], normed) * SCALE).astype(BF16)
    out_q = fetch(near_q, q_out, sems.at[8])
    outs = [head_output(scores[head], v[head]) for head in range(heads)]
    att_out[...] = jnp.concatenate(outs, axis=0).T.astype(BF16)
    for copy in (out_k, out_v, out_q):
        copy.wait()


def near_kernel(
    heads, q_hbm, k_hbm, v_hbm, tok_hbm, mods, w_hbm, part_out, q, k, v, tok, w, scores, sems
):
    in_q = fetch(q_hbm, q, sems.at[0])
    in_k = fetch(k_hbm, k, sems.at[1])
    in_v = fetch(v_hbm, v, sems.at[2])
    in_w = fetch(w_hbm, w, sems.at[3])
    in_tok = fetch(tok_hbm, tok, sems.at[4])
    in_q.wait()
    in_k.wait()
    queries = q[...].astype(F32)
    for head in range(heads):
        scores[head] = head_scores(queries, k, head)
    in_v.wait()
    outs = [head_output(scores[head], v[head]) for head in range(heads)]
    attended = jnp.concatenate(outs, axis=0).T.astype(BF16)
    in_w.wait()
    projected = jnp.dot(attended, w[...], preferred_element_type=F32)
    in_tok.wait()
    part_out[...] = tok[...].astype(F32) + mods[2:3] * projected


def piece_kernel(clip, first_hbm, second_hbm, after, out_hbm, piece, sems):
    rows = piece.shape[0]
    split = first_hbm.shape[0] // rows
    index = clip[0]

    @pl.when(index < split)
    def _():
        span = pl.ds(pl.multiple_of(index * rows, rows), rows)
        fetch(first_hbm.at[span], piece, sems.at[0]).wait()

    @pl.when(index >= split)
    def _():
        span = pl.ds(pl.multiple_of((index - split) * rows, rows), rows)
        fetch(second_hbm.at[span], piece, sems.at[0]).wait()

    fetch(piece, out_hbm, sems.at[1]).wait()


def middle_kernel(
    part_hbm, att, w_hbm, mods, next_mods, middle_hbm, normed_out, part, w, middle, sems
):
    in_w = fetch(w_hbm, w, sems.at[0])
    in_part = fetch(part_hbm, part, sems.at[1])
    in_w.wait()
    projected = jnp.dot(att[...], w[...], preferred_element_type=F32)
    in_part.wait()
    middle[...] = part[...] + mods[2:3] * projected
    copy = fetch(middle, middle_hbm, sems.at[2])
    normed_out[...] = normalise(middle[...], next_mods[0:1], next_mods[1:2])
    copy.wait()


def temporal_kernel(
    heads, positions, moved, own_hbm, other_hbm, att_out, w, k, scores, out, sems
):
    half = heads * HEAD_DIM
    count, width = moved.shape
    depth = count // positions
    groups = positions // 8
    block = depth * 8
    copies = []
    for part in range(3):
        for side, source in enumerate((own_hbm, other_hbm)):
            rows = pl.ds(side * half, half)
            copies.append(
                fetch(
                    source.at[pl.ds(part * half, half)],
                    w.at[part, rows],
                    sems.at[part * 2 + side],
                )
            )
    here = lax.rem(lax.broadcasted_iota(jnp.int32, (block, block), 0), 8)
    there = lax.rem(lax.broadcasted_iota(jnp.int32, (block, block), 1), 8)
    bias = jnp.where(here == there, 0.0, -1e30)
    grid = moved[...].astype(F32).reshape(depth, positions, width)
    tokens = jnp.concatenate(
        [grid[:, g * 8 : g * 8 + 8].reshape(block, width) for g in range(groups)], axis=0
    ).astype(BF16)
    copies[0].wait()
    copies[1].wait()
    queries = dot_nt(w[0], tokens) * SCALE
    copies[2].wait()
    copies[3].wait()
    k[...] = dot_nt(tokens, w[1]).astype(BF16)
    copies[4].wait()
    copies[5].wait()
    values = dot_nt(w[2], tokens)
    spans = [slice(g * block, (g + 1) * block) for g in range(groups)]
    for head in range(2 * heads):
        first, last = window(head)
        head_q = head_queries(queries, head)
        for g, span in enumerate(spans):
            scores[head * groups + g] = (
                jnp.dot(k[span, first:last], head_q[:, span], preferred_element_type=F32) + bias
            )
    for head in range(2 * heads):
        head_v = head_values(values, head)
        outs = [
            head_output(scores[head * groups + g], head_v[:, span])
            for g, span in enumerate(spans)
        ]
        out[pl.ds(head * HEAD_DIM, HEAD_DIM), :] = jnp.concatenate(outs, axis=1)
    result = out[...].T
    by_group = [result[span].reshape(depth, 8, 2 * half) for span in spans]
    att_out[...] = jnp.concatenate(by_group, axis=1).reshape(count, 2 * half).astype(BF16)


def final_kernel(att, own_w, other_w, middle_hbm, mods, out_hbm, w, middle, out, sems):
    half = own_w.shape[0]
    copies = [
        fetch(own_w, w.at[pl.ds(0, half)], sems.at[0]),
        fetch(other_w.at[pl.ds(3 * half, half)], w.at[pl.ds(half, half)], sems.at[1]),
        fetch(middle_hbm, middle, sems.at[2]),
    ]
    count, width = middle.shape
    tiles = width // LANES
    chunk = count // CHUNKS
    copies[0].wait()
    copies[1].wait()
    stores = []
    for part in range(CHUNKS):
        rows = pl.ds(part * chunk, chunk)
        projected = jnp.dot(att[rows, :], w[...], preferred_element_type=F32)
        if part == 0:
            copies[2].wait()
        result = middle[rows, :] + mods[2:3] * projected
        base = part * chunk * tiles
        for tile in range(tiles):
            out[pl.ds(base + tile, chunk, tiles), :] = result[
                :, tile * LANES : (tile + 1) * LANES
            ]
        span = pl.ds(base, chunk * tiles)
        stores.append(fetch(out.at[span], out_hbm.at[span], sems.at[3 + part]))
    for store in stores:
        store.wait()


def time_features(timestep):
    half = FREQ // 2
    ladder = jnp.exp(-math.log(10000.0) * jnp.arange(half, dtype=F32) / half)
    angles = timestep.astype(F32)[:, None] * ladder[None, :]
    return jnp.concatenate([jnp.cos(angles), jnp.sin(angles)], axis=-1)


def modulation_terms(timestep, embed_weight, block_weight):
    features = time_features(timestep)
    embedded = jax.nn.silu(
        jnp.dot(features, embed_weight.astype(F32), precision=lax.Precision.HIGHEST)
    )
    count, width = block_weight.shape
    start = lax.axis_index(("seq", "tp")) * count
    mine = lax.dynamic_slice_in_dim(embedded, start, count, 1)
    term = jnp.dot(mine, block_weight.astype(F32), precision=lax.Precision.HIGHEST)
    tiles = width // LANES
    return jnp.pad(term.reshape(tiles, LANES), ((0, TERM_ROWS - tiles), (0, 0)))


def follows(index, value):
    return index + (value.astype(F32) > 1e30).astype(jnp.int32)


def eighth(weight):
    rows = weight.shape[0] // lax.axis_size("clip")
    return lax.dynamic_slice_in_dim(weight, lax.axis_index("clip") * rows, rows, 0)


def body(
    frames,
    timestep,
    embed_weight,
    block_weight,
    spatial_table,
    temporal_table,
    spatial_qkv,
    spatial_out,
    temporal_qkv,
    temporal_out,
):
    width = frames.shape[-1]
    tokens = frames.reshape(-1, width)
    count = tokens.shape[0]
    half = spatial_out.shape[0]
    heads = half // HEAD_DIM
    far = lax.ppermute(tokens, "tp", SWAP)
    spatial_in = jnp.transpose(spatial_qkv, (1, 2, 0)).reshape(-1, width)
    temporal_in = jnp.transpose(temporal_qkv, (1, 2, 0)).reshape(-1, width)

    shape = jax.ShapeDtypeStruct
    dma = pltpu.SemaphoreType.DMA
    group = lax.axis_size("seq") * lax.axis_size("tp")
    across = [(i, i ^ 3) for i in range(group)]
    clip = lax.axis_index("clip")
    out_piece = lax.ppermute(eighth(spatial_out), ("seq", "tp"), across)
    term = modulation_terms(timestep, embed_weight, block_weight)
    copies = jnp.broadcast_to(term[None], (group,) + term.shape).reshape(-1, LANES)
    terms = lax.all_to_all(copies, ("seq", "tp"), 0, 0, tiled=True)
    spatial_out_other = lax.all_gather(out_piece, "clip", axis=0, tiled=True)
    rows = 4 * half // lax.axis_size("clip")
    own_piece = call(
        piece_kernel,
        shape((rows, width), BF16),
        [SMEM] + [HBM] * 3,
        [pltpu.VMEM((rows, width), BF16), dma((2,))],
        flops=20_000_000_000,
        nbytes=1_500_000,
        out_specs=HBM,
    )(clip.astype(jnp.int32).reshape(1), temporal_in, temporal_out, far)
    piece = lax.ppermute(own_piece, ("seq", "tp"), across)

    tokens_shape = (count, width)
    k_shape = (2 * count, padded(half))
    v_shape = (heads, HEAD_DIM + 8, 2 * count)
    all_scores = pltpu.VMEM((heads, 2 * count, count), F32)
    spatial_mods, temporal_mods, near_q, k, v, far_attended = call(
        functools.partial(spatial_kernel, heads),
        (
            shape((3, width), F32),
            shape((3, width), F32),
            shape((half, count), BF16),
            shape(k_shape, BF16),
            shape(v_shape, BF16),
            shape((count, half), BF16),
        ),
        [HBM] * 3 + [VMEM] * 2 + [HBM] * 2,
        [
            pltpu.VMEM(tokens_shape, BF16),
            pltpu.VMEM(tokens_shape, BF16),
            pltpu.VMEM(terms.shape, F32),
            pltpu.VMEM((3, half, width), BF16),
            pltpu.VMEM((half, count), F32),
            pltpu.VMEM((half, count), BF16),
            pltpu.VMEM(k_shape, BF16),
            pltpu.VMEM(v_shape, BF16),
            all_scores,
            dma((9,)),
        ],
        flops=14 * count * half * width,
        nbytes=14_000_000,
        out_specs=(VMEM, VMEM, HBM, HBM, HBM, VMEM),
    )(tokens, far, terms, spatial_table, temporal_table, spatial_in, own_piece)
    attended = lax.ppermute(far_attended, "tp", SWAP)
    late = follows(0, far_attended[0, 0]) > 0
    piece = jnp.where(late, jnp.zeros_like(piece), piece)
    gathered = lax.all_gather(piece, "clip", axis=0, tiled=True)
    part = call(
        functools.partial(near_kernel, heads),
        shape(tokens_shape, F32),
        [HBM] * 4 + [VMEM, HBM],
        [
            pltpu.VMEM((half, count), BF16),
            pltpu.VMEM(k_shape, BF16),
            pltpu.VMEM(v_shape, BF16),
            pltpu.VMEM(tokens_shape, BF16),
            pltpu.VMEM((half, width), BF16),
            all_scores,
            dma((5,)),
        ],
        flops=6 * count * half * width,
        nbytes=8_000_000,
    )(near_q, k, v, tokens, spatial_mods, spatial_out)
    middle, normed = call(
        middle_kernel,
        (shape(tokens_shape, F32), shape(tokens_shape, BF16)),
        [HBM, VMEM, HBM, VMEM, VMEM],
        [
            pltpu.VMEM(tokens_shape, F32),
            pltpu.VMEM((half, width), BF16),
            pltpu.VMEM(tokens_shape, F32),
            dma((3,)),
        ],
        flops=2 * count * half * width,
        nbytes=6_000_000,
        out_specs=(HBM, VMEM),
        mib=60,
    )(part, attended, spatial_out_other, spatial_mods, temporal_mods)

    moved = lax.all_to_all(normed, "seq", 0, 0, tiled=True)
    positions = count // lax.axis_size("seq")
    block = 8 * lax.axis_size("seq")
    attended = call(
        functools.partial(temporal_kernel, heads, positions),
        shape((count, 2 * half), BF16),
        [VMEM, HBM, HBM],
        [
            pltpu.VMEM((3, 2 * half, width), BF16),
            pltpu.VMEM((count, 2 * half), BF16),
            pltpu.VMEM((2 * heads * (positions // 8), block, block), F32),
            pltpu.VMEM((2 * half, count), F32),
            dma((6,)),
        ],
        flops=12 * count * half * width,
        nbytes=10_000_000,
        mib=60,
    )(moved, temporal_in, gathered)
    returned = lax.all_to_all(attended, "seq", 0, 0, tiled=True)
    tiles = width // LANES
    out = call(
        final_kernel,
        shape((count * tiles, LANES), F32),
        [VMEM, HBM, HBM, HBM, VMEM],
        [
            pltpu.VMEM((2 * half, width), BF16),
            pltpu.VMEM((count, width), F32),
            pltpu.VMEM((count * tiles, LANES), F32),
            dma((3 + CHUNKS,)),
        ],
        flops=4 * count * half * width,
        nbytes=8_000_000,
        out_specs=HBM,
        mib=60,
    )(returned, temporal_out, gathered, middle, temporal_mods)
    return out.reshape(frames.shape)


def solution(mesh):
    return jax.shard_map(
        body,
        mesh=mesh,
        in_specs=(
            P("tp", ("clip", "seq"), None),
            P("clip"),
            P(),
            P(("seq", "tp"), None),
            P(),
            P(),
            P(None, None, "tp"),
            P("tp", None),
            P(None, None, "tp"),
            P("tp", None),
        ),
        out_specs=P("tp", ("clip", "seq"), None),
        check_vma=False,
    )
```

```python
import functools
import math

import jax
import jax.numpy as jnp
from jax import lax
from jax.experimental import pallas as pl
from jax.experimental.pallas import tpu as pltpu
from jax.sharding import PartitionSpec as P

HEAD_DIM = 72
FREQ = 256
LANES = 128
SWAP = [(0, 1), (1, 0)]
VMEM = pl.BlockSpec(memory_space=pltpu.VMEM)
HBM = pl.BlockSpec(memory_space=pl.ANY)
TERM_ROWS = 32
CHUNKS = 2
SCALE = math.log2(math.e) / math.sqrt(HEAD_DIM)
BF16 = jnp.bfloat16
F32 = jnp.float32


def call(kernel, outs, in_specs, scratch=(), flops=0, nbytes=0, out_specs=None, mib=63.1):
    return pl.pallas_call(
        kernel,
        out_shape=outs,
        in_specs=in_specs,
        out_specs=out_specs or jax.tree.map(lambda _: VMEM, outs),
        scratch_shapes=list(scratch),
        compiler_params=pltpu.CompilerParams(vmem_limit_bytes=int(mib * 1024 * 1024)),
        cost_estimate=pl.CostEstimate(flops=flops, bytes_accessed=nbytes, transcendentals=0),
    )


def dot_nt(a, b):
    return lax.dot_general(a, b, (((1,), (1,)), ((), ())), preferred_element_type=F32)


def normalise(tokens, shift, scale):
    mean = jnp.mean(tokens, axis=-1, keepdims=True)
    centred = tokens - mean
    variance = jnp.mean(centred * centred, axis=-1, keepdims=True)
    return (centred * lax.rsqrt(variance + 1e-06) * (1.0 + scale) + shift).astype(BF16)


def fetch(source, target, sem):
    copy = pltpu.make_async_copy(source, target, sem)
    copy.start()
    return copy


def window(head):
    first = head * HEAD_DIM // LANES * LANES
    last = -(-(head + 1) * HEAD_DIM // LANES) * LANES
    return first, last


def padded(width):
    return -(-width // LANES) * LANES


def head_queries(queries, head):
    first, last = window(head)
    start = head * HEAD_DIM
    pieces = [queries[start : start + HEAD_DIM]]
    tokens = queries.shape[1]
    if start > first:
        pieces.insert(0, jnp.zeros((start - first, tokens), F32))
    if last > start + HEAD_DIM:
        pieces.append(jnp.zeros((last - start - HEAD_DIM, tokens), F32))
    return jnp.concatenate(pieces, axis=0).astype(BF16)


def head_values(values, head):
    start = head * HEAD_DIM
    ones = jnp.ones((8, values.shape[1]), F32)
    return jnp.concatenate([values[start : start + HEAD_DIM], ones], axis=0).astype(BF16)


def head_scores(queries, keys, head):
    first, last = window(head)
    return jnp.dot(keys[:, first:last], head_queries(queries, head), preferred_element_type=F32)


def head_output(scores, values):
    peak = jnp.max(scores, axis=0, keepdims=True)
    raised = jnp.exp2(scores - peak).astype(BF16)
    out = jnp.dot(values, raised, preferred_element_type=F32)
    return out[:HEAD_DIM] / out[HEAD_DIM : HEAD_DIM + 1]


def modulation_table(terms, table):
    group = terms.shape[0] // TERM_ROWS
    total = jnp.sum(terms[...].reshape(group, TERM_ROWS, LANES), axis=0)
    tiles = table.shape[1] // LANES
    rows = []
    for row in range(3):
        parts = [total[row * tiles + t : row * tiles + t + 1] for t in range(tiles)]
        rows.append(jnp.concatenate(parts, axis=1))
    return jnp.concatenate(rows, axis=0)


def fetch_parts(w_hbm, w, sems):
    half = w.shape[1]
    return [fetch(w_hbm.at[pl.ds(p * half, half)], w.at[p], sems.at[p]) for p in range(3)]


def spatial_kernel(
    heads,
    tok_hbm,
    far_hbm,
    terms_hbm,
    table,
    next_table,
    w_hbm,
    after,
    mods_out,
    next_out,
    normed_out,
    k_out,
    v_out,
    att_out,
    tok,
    far,
    terms,
    w,
    q,
    k,
    v,
    scores,
    sems,
):
    count, half = far.shape[0], heads * HEAD_DIM
    in_terms = fetch(terms_hbm, terms, sems.at[3])
    in_far = fetch(far_hbm, far, sems.at[4])
    in_w = fetch_parts(w_hbm, w, sems)
    in_tok = fetch(tok_hbm, tok, sems.at[5])
    near, beyond = pl.ds(0, count), pl.ds(count, count)
    k[:, k.shape[1] - LANES :] = jnp.zeros((2 * count, LANES), BF16)
    in_terms.wait()
    modulation = modulation_table(terms, table)
    mods = table[...] + modulation
    mods_out[...] = mods
    next_out[...] = next_table[...] + modulation
    in_far.wait()
    normed_far = normalise(far[...].astype(F32), mods[0:1], mods[1:2])
    in_w[0].wait()
    q[...] = dot_nt(w[0], normed_far) * SCALE
    in_w[1].wait()
    k[beyond, :half] = dot_nt(normed_far, w[1]).astype(BF16)
    in_tok.wait()
    normed = normalise(tok[...].astype(F32), mods[0:1], mods[1:2])
    tok[...] = normed
    out_normed = fetch(tok, normed_out, sems.at[8])
    k[near, :half] = dot_nt(normed, w[1]).astype(BF16)
    out_k = fetch(k, k_out, sems.at[6])
    for head in range(heads):
        scores[head] = head_scores(q, k, head)
    in_w[2].wait()
    values = dot_nt(w[2], normed)
    for head in range(heads):
        v[head, :, :count] = head_values(values, head)
    values = dot_nt(w[2], normed_far)
    for head in range(heads):
        v[head, :, count:] = head_values(values, head)
    out_v = fetch(v, v_out, sems.at[7])
    outs = [head_output(scores[head], v[head]) for head in range(heads)]
    att_out[...] = jnp.concatenate(outs, axis=0).T.astype(BF16)
    for copy in (out_k, out_v, out_normed):
        copy.wait()


def near_kernel(
    heads,
    normed_hbm,
    in_w_hbm,
    k_hbm,
    v_hbm,
    tok_hbm,
    mods,
    w_hbm,
    part_out,
    normed,
    in_w,
    k,
    v,
    tok,
    w,
    scores,
    sems,
):
    half = heads * HEAD_DIM
    copies = [
        fetch(normed_hbm, normed, sems.at[0]),
        fetch(in_w_hbm.at[pl.ds(0, half)], in_w, sems.at[1]),
        fetch(k_hbm, k, sems.at[2]),
        fetch(v_hbm, v, sems.at[3]),
        fetch(w_hbm, w, sems.at[4]),
        fetch(tok_hbm, tok, sems.at[5]),
    ]
    copies[0].wait()
    copies[1].wait()
    queries = dot_nt(in_w[...], normed[...]) * SCALE
    copies[2].wait()
    for head in range(heads):
        scores[head] = head_scores(queries, k, head)
    copies[3].wait()
    outs = [head_output(scores[head], v[head]) for head in range(heads)]
    attended = jnp.concatenate(outs, axis=0).T.astype(BF16)
    copies[4].wait()
    projected = jnp.dot(attended, w[...], preferred_element_type=F32)
    copies[5].wait()
    part_out[...] = tok[...].astype(F32) + mods[2:3] * projected


def piece_kernel(own_hbm, after, out_hbm, piece, sems):
    fetch(own_hbm, piece, sems.at[0]).wait()
    fetch(piece, out_hbm, sems.at[1]).wait()


def middle_kernel(
    part_hbm, att, w_hbm, mods, next_mods, middle_hbm, normed_out, part, w, middle, sems
):
    in_w = fetch(w_hbm, w, sems.at[0])
    in_part = fetch(part_hbm, part, sems.at[1])
    in_w.wait()
    projected = jnp.dot(att[...], w[...], preferred_element_type=F32)
    in_part.wait()
    middle[...] = part[...] + mods[2:3] * projected
    copy = fetch(middle, middle_hbm, sems.at[2])
    normed_out[...] = normalise(middle[...], next_mods[0:1], next_mods[1:2])
    copy.wait()


def temporal_kernel(
    heads, positions, moved, own_hbm, other_hbm, att_out, w, k, scores, out, sems
):
    half = heads * HEAD_DIM
    count, width = moved.shape
    depth = count // positions
    groups = positions // 8
    block = depth * 8
    copies = []
    for part in range(3):
        for side, source in enumerate((own_hbm, other_hbm)):
            rows = pl.ds(side * half, half)
            copies.append(
                fetch(
                    source.at[pl.ds(part * half, half)],
                    w.at[part, rows],
                    sems.at[part * 2 + side],
                )
            )
    here = lax.rem(lax.broadcasted_iota(jnp.int32, (block, block), 0), 8)
    there = lax.rem(lax.broadcasted_iota(jnp.int32, (block, block), 1), 8)
    bias = jnp.where(here == there, 0.0, -1e30)
    grid = moved[...].astype(F32).reshape(depth, positions, width)
    tokens = jnp.concatenate(
        [grid[:, g * 8 : g * 8 + 8].reshape(block, width) for g in range(groups)], axis=0
    ).astype(BF16)
    copies[0].wait()
    copies[1].wait()
    queries = dot_nt(w[0], tokens) * SCALE
    copies[2].wait()
    copies[3].wait()
    k[...] = dot_nt(tokens, w[1]).astype(BF16)
    spans = [slice(g * block, (g + 1) * block) for g in range(groups)]
    for head in range(2 * heads):
        first, last = window(head)
        head_q = head_queries(queries, head)
        for g, span in enumerate(spans):
            scores[head * groups + g] = (
                jnp.dot(k[span, first:last], head_q[:, span], preferred_element_type=F32) + bias
            )
    copies[4].wait()
    copies[5].wait()
    values = dot_nt(w[2], tokens)
    for head in range(2 * heads):
        head_v = head_values(values, head)
        outs = [
            head_output(scores[head * groups + g], head_v[:, span])
            for g, span in enumerate(spans)
        ]
        out[pl.ds(head * HEAD_DIM, HEAD_DIM), :] = jnp.concatenate(outs, axis=1)
    result = out[...].T
    by_group = [result[span].reshape(depth, 8, 2 * half) for span in spans]
    att_out[...] = jnp.concatenate(by_group, axis=1).reshape(count, 2 * half).astype(BF16)


def final_kernel(att, own_w, other_w, middle_hbm, mods, out_hbm, w, middle, out, sems):
    half = own_w.shape[0]
    copies = [
        fetch(own_w, w.at[pl.ds(0, half)], sems.at[0]),
        fetch(other_w, w.at[pl.ds(half, half)], sems.at[1]),
        fetch(middle_hbm, middle, sems.at[2]),
    ]
    count, width = middle.shape
    tiles = width // LANES
    chunk = count // CHUNKS
    split = half // LANES * LANES
    copies[0].wait()
    early = jnp.dot(att[:, :split], w[:split, :], preferred_element_type=F32)
    copies[1].wait()
    stores = []
    for part in range(CHUNKS):
        rows = pl.ds(part * chunk, chunk)
        projected = early[part * chunk : (part + 1) * chunk]
        projected += jnp.dot(att[rows, split:], w[split:, :], preferred_element_type=F32)
        if part == 0:
            copies[2].wait()
        result = middle[rows, :] + mods[2:3] * projected
        base = part * chunk * tiles
        for tile in range(tiles):
            out[pl.ds(base + tile, chunk, tiles), :] = result[
                :, tile * LANES : (tile + 1) * LANES
            ]
        span = pl.ds(base, chunk * tiles)
        stores.append(fetch(out.at[span], out_hbm.at[span], sems.at[3 + part]))
    for store in stores:
        store.wait()


def time_features(timestep):
    half = FREQ // 2
    ladder = jnp.exp(-math.log(10000.0) * jnp.arange(half, dtype=F32) / half)
    angles = timestep.astype(F32)[:, None] * ladder[None, :]
    return jnp.concatenate([jnp.cos(angles), jnp.sin(angles)], axis=-1)


def modulation_terms(timestep, embed_weight, block_weight):
    features = time_features(timestep)
    embedded = jax.nn.silu(
        jnp.dot(features, embed_weight.astype(F32), precision=lax.Precision.HIGHEST)
    )
    count, width = block_weight.shape
    start = lax.axis_index(("seq", "tp")) * count
    mine = lax.dynamic_slice_in_dim(embedded, start, count, 1)
    term = jnp.dot(mine, block_weight.astype(F32), precision=lax.Precision.HIGHEST)
    tiles = width // LANES
    return jnp.pad(term.reshape(tiles, LANES), ((0, TERM_ROWS - tiles), (0, 0)))


def eighth(weight):
    rows = weight.shape[0] // lax.axis_size("clip")
    return lax.dynamic_slice_in_dim(weight, lax.axis_index("clip") * rows, rows, 0)


def body(
    frames,
    timestep,
    embed_weight,
    block_weight,
    spatial_table,
    temporal_table,
    spatial_qkv,
    spatial_out,
    temporal_qkv,
    temporal_out,
):
    width = frames.shape[-1]
    tokens = frames.reshape(-1, width)
    count = tokens.shape[0]
    half = spatial_out.shape[0]
    heads = half // HEAD_DIM
    far = lax.ppermute(tokens, "tp", SWAP)
    spatial_in = jnp.transpose(spatial_qkv, (1, 2, 0)).reshape(-1, width)
    temporal_in = jnp.transpose(temporal_qkv, (1, 2, 0)).reshape(-1, width)

    shape = jax.ShapeDtypeStruct
    dma = pltpu.SemaphoreType.DMA
    group = lax.axis_size("seq") * lax.axis_size("tp")
    across = [(i, i ^ 3) for i in range(group)]
    out_piece = lax.ppermute(eighth(spatial_out), ("seq", "tp"), across)
    term = modulation_terms(timestep, embed_weight, block_weight)
    copies = jnp.broadcast_to(term[None], (group,) + term.shape).reshape(-1, LANES)
    terms = lax.all_to_all(copies, ("seq", "tp"), 0, 0, tiled=True)
    own_piece = eighth(temporal_in)
    own_piece = call(
        piece_kernel,
        shape(own_piece.shape, BF16),
        [HBM] * 2,
        [pltpu.VMEM(own_piece.shape, BF16), dma((2,))],
        flops=20_000_000_000,
        nbytes=1_500_000,
        out_specs=HBM,
    )(own_piece, far)
    out_piece, _ = lax.optimization_barrier((out_piece, (own_piece, terms)))
    spatial_out_other = lax.all_gather(out_piece, "clip", axis=0, tiled=True)
    piece = lax.ppermute(own_piece, ("seq", "tp"), across)

    tokens_shape = (count, width)
    k_shape = (2 * count, padded(half))
    v_shape = (heads, HEAD_DIM + 8, 2 * count)
    all_scores = pltpu.VMEM((heads, 2 * count, count), F32)
    spatial_mods, temporal_mods, normed, k, v, far_attended = call(
        functools.partial(spatial_kernel, heads),
        (
            shape((3, width), F32),
            shape((3, width), F32),
            shape(tokens_shape, BF16),
            shape(k_shape, BF16),
            shape(v_shape, BF16),
            shape((count, half), BF16),
        ),
        [HBM] * 3 + [VMEM] * 2 + [HBM] * 2,
        [
            pltpu.VMEM(tokens_shape, BF16),
            pltpu.VMEM(tokens_shape, BF16),
            pltpu.VMEM(terms.shape, F32),
            pltpu.VMEM((3, half, width), BF16),
            pltpu.VMEM((half, count), F32),
            pltpu.VMEM(k_shape, BF16),
            pltpu.VMEM(v_shape, BF16),
            all_scores,
            dma((9,)),
        ],
        flops=14 * count * half * width,
        nbytes=14_000_000,
        out_specs=(VMEM, VMEM, HBM, HBM, HBM, VMEM),
        mib=63.1,
    )(tokens, far, terms, spatial_table, temporal_table, spatial_in, own_piece)
    attended = lax.ppermute(far_attended, "tp", SWAP)
    part = call(
        functools.partial(near_kernel, heads),
        shape(tokens_shape, F32),
        [HBM] * 5 + [VMEM, HBM],
        [
            pltpu.VMEM(tokens_shape, BF16),
            pltpu.VMEM((half, width), BF16),
            pltpu.VMEM(k_shape, BF16),
            pltpu.VMEM(v_shape, BF16),
            pltpu.VMEM(tokens_shape, BF16),
            pltpu.VMEM((half, width), BF16),
            all_scores,
            dma((6,)),
        ],
        flops=6 * count * half * width,
        nbytes=8_000_000,
        mib=63.1,
    )(normed, spatial_in, k, v, tokens, spatial_mods, spatial_out)
    piece, _ = lax.optimization_barrier((piece, (attended, part)))
    temporal_in_other = lax.all_gather(piece, "clip", axis=0, tiled=True)
    middle, normed = call(
        middle_kernel,
        (shape(tokens_shape, F32), shape(tokens_shape, BF16)),
        [HBM, VMEM, HBM, VMEM, VMEM],
        [
            pltpu.VMEM(tokens_shape, F32),
            pltpu.VMEM((half, width), BF16),
            pltpu.VMEM(tokens_shape, F32),
            dma((3,)),
        ],
        flops=2 * count * half * width,
        nbytes=6_000_000,
        out_specs=(HBM, VMEM),
        mib=63.1,
    )(part, attended, spatial_out_other, spatial_mods, temporal_mods)

    out_piece, _ = lax.optimization_barrier((eighth(temporal_out), normed))
    out_piece = lax.ppermute(out_piece, ("seq", "tp"), across)
    temporal_out_other = lax.all_gather(out_piece, "clip", axis=0, tiled=True)
    moved = lax.all_to_all(normed, "seq", 0, 0, tiled=True)
    positions = count // lax.axis_size("seq")
    block = 8 * lax.axis_size("seq")
    attended = call(
        functools.partial(temporal_kernel, heads, positions),
        shape((count, 2 * half), BF16),
        [VMEM, HBM, HBM],
        [
            pltpu.VMEM((3, 2 * half, width), BF16),
            pltpu.VMEM((count, 2 * half), BF16),
            pltpu.VMEM((2 * heads * (positions // 8), block, block), F32),
            pltpu.VMEM((2 * half, count), F32),
            dma((6,)),
        ],
        flops=12 * count * half * width,
        nbytes=10_000_000,
        mib=63.1,
    )(moved, temporal_in, temporal_in_other)
    returned = lax.all_to_all(attended, "seq", 0, 0, tiled=True)
    tiles = width // LANES
    out = call(
        final_kernel,
        shape((count * tiles, LANES), F32),
        [VMEM, HBM, HBM, HBM, VMEM],
        [
            pltpu.VMEM((2 * half, width), BF16),
            pltpu.VMEM((count, width), F32),
            pltpu.VMEM((count * tiles, LANES), F32),
            dma((3 + CHUNKS,)),
        ],
        flops=4 * count * half * width,
        nbytes=8_000_000,
        out_specs=HBM,
        mib=63.1,
    )(returned, temporal_out, temporal_out_other, middle, temporal_mods)
    return out.reshape(frames.shape)


def solution(mesh):
    return jax.shard_map(
        body,
        mesh=mesh,
        in_specs=(
            P("tp", ("clip", "seq"), None),
            P("clip"),
            P(),
            P(("seq", "tp"), None),
            P(),
            P(),
            P(None, None, "tp"),
            P("tp", None),
            P(None, None, "tp"),
            P("tp", None),
        ),
        out_specs=P("tp", ("clip", "seq"), None),
        check_vma=False,
    )
```

```python
import functools
import math

import jax
import jax.numpy as jnp
from jax import lax
from jax.experimental import pallas as pl
from jax.experimental.pallas import tpu as pltpu
from jax.sharding import PartitionSpec as P

HEAD_DIM = 72
FREQ = 256
LANES = 128
SWAP = [(0, 1), (1, 0)]
VMEM = pl.BlockSpec(memory_space=pltpu.VMEM)
HBM = pl.BlockSpec(memory_space=pl.ANY)
TERM_ROWS = 32
CHUNKS = 4
SCALE = math.log2(math.e) / math.sqrt(HEAD_DIM)
BF16 = jnp.bfloat16
F32 = jnp.float32


def call(kernel, outs, in_specs, scratch=(), flops=0, nbytes=0, out_specs=None, mib=63.1):
    return pl.pallas_call(
        kernel,
        out_shape=outs,
        in_specs=in_specs,
        out_specs=out_specs or jax.tree.map(lambda _: VMEM, outs),
        scratch_shapes=list(scratch),
        compiler_params=pltpu.CompilerParams(vmem_limit_bytes=int(mib * 1024 * 1024)),
        cost_estimate=pl.CostEstimate(flops=flops, bytes_accessed=nbytes, transcendentals=0),
    )


def dot_nt(a, b):
    return lax.dot_general(a, b, (((1,), (1,)), ((), ())), preferred_element_type=F32)


def normalise(tokens, shift, scale):
    mean = jnp.mean(tokens, axis=-1, keepdims=True)
    centred = tokens - mean
    variance = jnp.mean(centred * centred, axis=-1, keepdims=True)
    return (centred * lax.rsqrt(variance + 1e-06) * (1.0 + scale) + shift).astype(BF16)


def fetch(source, target, sem):
    copy = pltpu.make_async_copy(source, target, sem)
    copy.start()
    return copy


def window(head):
    first = head * HEAD_DIM // LANES * LANES
    last = -(-(head + 1) * HEAD_DIM // LANES) * LANES
    return first, last


def padded(width):
    return -(-width // LANES) * LANES


def head_queries(queries, head):
    first, last = window(head)
    start = head * HEAD_DIM
    pieces = [queries[start : start + HEAD_DIM]]
    tokens = queries.shape[1]
    if start > first:
        pieces.insert(0, jnp.zeros((start - first, tokens), F32))
    if last > start + HEAD_DIM:
        pieces.append(jnp.zeros((last - start - HEAD_DIM, tokens), F32))
    return jnp.concatenate(pieces, axis=0).astype(BF16)


def head_values(values, head):
    start = head * HEAD_DIM
    ones = jnp.ones((8, values.shape[1]), F32)
    return jnp.concatenate([values[start : start + HEAD_DIM], ones], axis=0).astype(BF16)


def head_scores(queries, keys, head):
    first, last = window(head)
    return jnp.dot(keys[:, first:last], head_queries(queries, head), preferred_element_type=F32)


def head_output(scores, values):
    peak = jnp.max(scores, axis=0, keepdims=True)
    raised = jnp.exp2(scores - peak).astype(BF16)
    out = jnp.dot(values, raised, preferred_element_type=F32)
    return out[:HEAD_DIM] / out[HEAD_DIM : HEAD_DIM + 1]


def modulation_table(total, table):
    tiles = table.shape[1] // LANES
    rows = []
    for row in range(3):
        parts = [total[row * tiles + t : row * tiles + t + 1] for t in range(tiles)]
        rows.append(jnp.concatenate(parts, axis=1))
    return jnp.concatenate(rows, axis=0)


def fetch_parts(w_hbm, w, sems):
    half = w.shape[1]
    return [fetch(w_hbm.at[pl.ds(p * half, half)], w.at[p], sems.at[p]) for p in range(3)]


def spatial_kernel(
    heads,
    tok_hbm,
    far_hbm,
    own_total,
    other_total,
    table,
    next_table,
    w_hbm,
    after,
    mods_out,
    next_out,
    normed_out,
    k_out,
    v_out,
    att_out,
    tok,
    far,
    w,
    q,
    k,
    v,
    scores,
    sems,
):
    count, half = far.shape[0], heads * HEAD_DIM
    in_far = fetch(far_hbm, far, sems.at[4])
    in_w = fetch_parts(w_hbm, w, sems)
    in_tok = fetch(tok_hbm, tok, sems.at[5])
    near, beyond = pl.ds(0, count), pl.ds(count, count)
    k[:, k.shape[1] - LANES :] = jnp.zeros((2 * count, LANES), BF16)
    modulation = modulation_table(own_total[...] + other_total[...], table)
    mods = table[...] + modulation
    mods_out[...] = mods
    next_out[...] = next_table[...] + modulation
    in_far.wait()
    normed_far = normalise(far[...].astype(F32), mods[0:1], mods[1:2])
    in_w[0].wait()
    q[...] = dot_nt(w[0], normed_far) * SCALE
    in_w[1].wait()
    k[beyond, :half] = dot_nt(normed_far, w[1]).astype(BF16)
    in_tok.wait()
    normed = normalise(tok[...].astype(F32), mods[0:1], mods[1:2])
    tok[...] = normed
    out_normed = fetch(tok, normed_out, sems.at[8])
    k[near, :half] = dot_nt(normed, w[1]).astype(BF16)
    out_k = fetch(k, k_out, sems.at[6])
    for head in range(heads):
        scores[head] = head_scores(q, k, head)
    in_w[2].wait()
    values = dot_nt(w[2], normed)
    for head in range(heads):
        v[head, :, :count] = head_values(values, head)
    values = dot_nt(w[2], normed_far)
    for head in range(heads):
        v[head, :, count:] = head_values(values, head)
    out_v = fetch(v, v_out, sems.at[7])
    outs = [head_output(scores[head], v[head]) for head in range(heads)]
    att_out[...] = jnp.concatenate(outs, axis=0).T.astype(BF16)
    for copy in (out_k, out_v, out_normed):
        copy.wait()


def near_kernel(
    heads,
    normed_hbm,
    in_w_hbm,
    k_hbm,
    v_hbm,
    tok_hbm,
    mods,
    w_hbm,
    part_out,
    normed,
    in_w,
    k,
    v,
    tok,
    w,
    scores,
    sems,
):
    half = heads * HEAD_DIM
    copies = [
        fetch(normed_hbm, normed, sems.at[0]),
        fetch(in_w_hbm.at[pl.ds(0, half)], in_w, sems.at[1]),
        fetch(k_hbm, k, sems.at[2]),
        fetch(v_hbm, v, sems.at[3]),
        fetch(w_hbm, w, sems.at[4]),
        fetch(tok_hbm, tok, sems.at[5]),
    ]
    copies[0].wait()
    copies[1].wait()
    queries = dot_nt(in_w[...], normed[...]) * SCALE
    copies[2].wait()
    for head in range(heads):
        scores[head] = head_scores(queries, k, head)
    copies[3].wait()
    outs = [head_output(scores[head], v[head]) for head in range(heads)]
    attended = jnp.concatenate(outs, axis=0).T.astype(BF16)
    copies[4].wait()
    projected = jnp.dot(attended, w[...], preferred_element_type=F32)
    copies[5].wait()
    part_out[...] = tok[...].astype(F32) + mods[2:3] * projected


def piece_kernel(own_hbm, after, out_hbm, piece, sems):
    fetch(own_hbm, piece, sems.at[0]).wait()
    fetch(piece, out_hbm, sems.at[1]).wait()


def middle_kernel(
    part_hbm, att_hbm, w_hbm, mods, next_mods, middle_hbm, normed_out, part, att, w, middle, sems
):
    in_w = fetch(w_hbm, w, sems.at[0])
    in_att = fetch(att_hbm, att, sems.at[3])
    in_part = fetch(part_hbm, part, sems.at[1])
    in_w.wait()
    in_att.wait()
    projected = jnp.dot(att[...], w[...], preferred_element_type=F32)
    in_part.wait()
    middle[...] = part[...] + mods[2:3] * projected
    copy = fetch(middle, middle_hbm, sems.at[2])
    normed_out[...] = normalise(middle[...], next_mods[0:1], next_mods[1:2])
    copy.wait()


def temporal_kernel(
    heads, positions, moved_hbm, own_hbm, other_hbm, att_out, moved, w, k, scores, out, sems
):
    half = heads * HEAD_DIM
    in_moved = fetch(moved_hbm, moved, sems.at[6])
    count, width = moved.shape
    depth = count // positions
    groups = positions // 8
    block = depth * 8
    copies = []
    for part in range(3):
        for side, source in enumerate((own_hbm, other_hbm)):
            rows = pl.ds(side * half, half)
            copies.append(
                fetch(
                    source.at[pl.ds(part * half, half)],
                    w.at[part, rows],
                    sems.at[part * 2 + side],
                )
            )
    here = lax.rem(lax.broadcasted_iota(jnp.int32, (block, block), 0), 8)
    there = lax.rem(lax.broadcasted_iota(jnp.int32, (block, block), 1), 8)
    bias = jnp.where(here == there, 0.0, -1e30)
    in_moved.wait()
    grid = moved[...].astype(F32).reshape(depth, positions, width)
    tokens = jnp.concatenate(
        [grid[:, g * 8 : g * 8 + 8].reshape(block, width) for g in range(groups)], axis=0
    ).astype(BF16)
    copies[0].wait()
    copies[1].wait()
    queries = dot_nt(w[0], tokens) * SCALE
    copies[2].wait()
    copies[3].wait()
    k[...] = dot_nt(tokens, w[1]).astype(BF16)
    spans = [slice(g * block, (g + 1) * block) for g in range(groups)]
    for head in range(2 * heads):
        first, last = window(head)
        head_q = head_queries(queries, head)
        for g, span in enumerate(spans):
            scores[head * groups + g] = (
                jnp.dot(k[span, first:last], head_q[:, span], preferred_element_type=F32) + bias
            )
    copies[4].wait()
    copies[5].wait()
    values = dot_nt(w[2], tokens)
    for head in range(2 * heads):
        head_v = head_values(values, head)
        outs = [
            head_output(scores[head * groups + g], head_v[:, span])
            for g, span in enumerate(spans)
        ]
        out[pl.ds(head * HEAD_DIM, HEAD_DIM), :] = jnp.concatenate(outs, axis=1)
    result = out[...].T
    by_group = [result[span].reshape(depth, 8, 2 * half) for span in spans]
    att_out[...] = jnp.concatenate(by_group, axis=1).reshape(count, 2 * half).astype(BF16)


def final_kernel(
    att_hbm, own_w, other_w, middle_hbm, mods, out_hbm, att, w, middle, out, sems
):
    half = own_w.shape[0]
    in_att = fetch(att_hbm, att, sems.at[3 + CHUNKS])
    copies = [
        fetch(own_w, w.at[pl.ds(0, half)], sems.at[0]),
        fetch(other_w, w.at[pl.ds(half, half)], sems.at[1]),
        fetch(middle_hbm, middle, sems.at[2]),
    ]
    count, width = middle.shape
    tiles = width // LANES
    chunk = count // CHUNKS
    split = half // LANES * LANES
    in_att.wait()
    copies[0].wait()
    early = jnp.dot(att[:, :split], w[:split, :], preferred_element_type=F32)
    copies[1].wait()
    stores = []
    for part in range(CHUNKS):
        rows = pl.ds(part * chunk, chunk)
        projected = early[part * chunk : (part + 1) * chunk]
        projected += jnp.dot(att[rows, split:], w[split:, :], preferred_element_type=F32)
        if part == 0:
            copies[2].wait()
        result = middle[rows, :] + mods[2:3] * projected
        base = part * chunk * tiles
        for tile in range(tiles):
            out[pl.ds(base + tile, chunk, tiles), :] = result[
                :, tile * LANES : (tile + 1) * LANES
            ]
        span = pl.ds(base, chunk * tiles)
        stores.append(fetch(out.at[span], out_hbm.at[span], sems.at[3 + part]))
    for store in stores:
        store.wait()


def time_features(timestep):
    half = FREQ // 2
    ladder = jnp.exp(-math.log(10000.0) * jnp.arange(half, dtype=F32) / half)
    angles = timestep.astype(F32)[:, None] * ladder[None, :]
    return jnp.concatenate([jnp.cos(angles), jnp.sin(angles)], axis=-1)


def modulation_terms(timestep, embed_weight, block_weight):
    features = time_features(timestep)
    embedded = jax.nn.silu(
        jnp.dot(features, embed_weight.astype(F32), precision=lax.Precision.HIGHEST)
    )
    count, width = block_weight.shape
    start = lax.axis_index(("seq", "tp")) * count
    mine = lax.dynamic_slice_in_dim(embedded, start, count, 1)
    term = jnp.dot(mine, block_weight.astype(F32), precision=lax.Precision.HIGHEST)
    tiles = width // LANES
    return jnp.pad(term.reshape(tiles, LANES), ((0, TERM_ROWS - tiles), (0, 0)))


def eighth(weight):
    rows = weight.shape[0] // lax.axis_size("clip")
    return lax.dynamic_slice_in_dim(weight, lax.axis_index("clip") * rows, rows, 0)


def body(
    frames,
    timestep,
    embed_weight,
    block_weight,
    spatial_table,
    temporal_table,
    spatial_qkv,
    spatial_out,
    temporal_qkv,
    temporal_out,
):
    width = frames.shape[-1]
    tokens = frames.reshape(-1, width)
    count = tokens.shape[0]
    half = spatial_out.shape[0]
    heads = half // HEAD_DIM
    far = lax.ppermute(tokens, "tp", SWAP)
    spatial_in = jnp.transpose(spatial_qkv, (1, 2, 0)).reshape(-1, width)
    temporal_in = jnp.transpose(temporal_qkv, (1, 2, 0)).reshape(-1, width)

    shape = jax.ShapeDtypeStruct
    dma = pltpu.SemaphoreType.DMA
    group = lax.axis_size("seq") * lax.axis_size("tp")
    across = [(i, i ^ 3) for i in range(group)]
    out_piece = lax.ppermute(eighth(spatial_out), ("seq", "tp"), across)
    term = modulation_terms(timestep, embed_weight, block_weight)
    copies = jnp.broadcast_to(term[None], (lax.axis_size("seq"),) + term.shape)
    terms = lax.all_to_all(copies.reshape(-1, LANES), "seq", 0, 0, tiled=True)
    own_total = jnp.sum(terms.reshape(copies.shape), axis=0)
    other_total = lax.ppermute(own_total, "tp", SWAP)
    own_piece = eighth(temporal_in)
    own_piece = call(
        piece_kernel,
        shape(own_piece.shape, BF16),
        [HBM] * 2,
        [pltpu.VMEM(own_piece.shape, BF16), dma((2,))],
        flops=20_000_000_000,
        nbytes=1_500_000,
        out_specs=HBM,
    )(own_piece, far)
    out_piece, _ = lax.optimization_barrier((out_piece, (own_total, far)))
    spatial_out_other = lax.all_gather(out_piece, "clip", axis=0, tiled=True)
    piece = lax.ppermute(own_piece, ("seq", "tp"), across)

    tokens_shape = (count, width)
    k_shape = (2 * count, padded(half))
    v_shape = (heads, HEAD_DIM + 8, 2 * count)
    all_scores = pltpu.VMEM((heads, 2 * count, count), F32)
    spatial_mods, temporal_mods, normed, k, v, far_attended = call(
        functools.partial(spatial_kernel, heads),
        (
            shape((3, width), F32),
            shape((3, width), F32),
            shape(tokens_shape, BF16),
            shape(k_shape, BF16),
            shape(v_shape, BF16),
            shape((count, half), BF16),
        ),
        [HBM] * 2 + [VMEM] * 4 + [HBM] * 2,
        [
            pltpu.VMEM(tokens_shape, BF16),
            pltpu.VMEM(tokens_shape, BF16),
            pltpu.VMEM((3, half, width), BF16),
            pltpu.VMEM((half, count), F32),
            pltpu.VMEM(k_shape, BF16),
            pltpu.VMEM(v_shape, BF16),
            all_scores,
            dma((9,)),
        ],
        flops=14 * count * half * width,
        nbytes=14_000_000,
        out_specs=(VMEM, VMEM, HBM, HBM, HBM, VMEM),
        mib=63.1,
    )(tokens, far, own_total, other_total, spatial_table, temporal_table, spatial_in, own_piece)
    attended = lax.ppermute(far_attended, "tp", SWAP)
    part = call(
        functools.partial(near_kernel, heads),
        shape(tokens_shape, F32),
        [HBM] * 5 + [VMEM, HBM],
        [
            pltpu.VMEM(tokens_shape, BF16),
            pltpu.VMEM((half, width), BF16),
            pltpu.VMEM(k_shape, BF16),
            pltpu.VMEM(v_shape, BF16),
            pltpu.VMEM(tokens_shape, BF16),
            pltpu.VMEM((half, width), BF16),
            all_scores,
            dma((6,)),
        ],
        flops=6 * count * half * width,
        nbytes=8_000_000,
        mib=63.1,
    )(normed, spatial_in, k, v, tokens, spatial_mods, spatial_out)
    piece, _ = lax.optimization_barrier((piece, (attended, part)))
    temporal_in_other = lax.all_gather(piece, "clip", axis=0, tiled=True)
    middle, normed = call(
        middle_kernel,
        (shape(tokens_shape, F32), shape(tokens_shape, BF16)),
        [HBM] * 3 + [VMEM] * 2,
        [
            pltpu.VMEM(tokens_shape, F32),
            pltpu.VMEM((count, half), BF16),
            pltpu.VMEM((half, width), BF16),
            pltpu.VMEM(tokens_shape, F32),
            dma((4,)),
        ],
        flops=2 * count * half * width,
        nbytes=6_000_000,
        out_specs=(HBM, VMEM),
        mib=63.1,
    )(part, attended, spatial_out_other, spatial_mods, temporal_mods)

    out_piece, _ = lax.optimization_barrier((eighth(temporal_out), normed))
    out_piece = lax.ppermute(out_piece, ("seq", "tp"), across)
    temporal_out_other = lax.all_gather(out_piece, "clip", axis=0, tiled=True)
    moved = lax.all_to_all(normed, "seq", 0, 0, tiled=True)
    positions = count // lax.axis_size("seq")
    block = 8 * lax.axis_size("seq")
    attended = call(
        functools.partial(temporal_kernel, heads, positions),
        shape((count, 2 * half), BF16),
        [HBM] * 3,
        [
            pltpu.VMEM(tokens_shape, BF16),
            pltpu.VMEM((3, 2 * half, width), BF16),
            pltpu.VMEM((count, 2 * half), BF16),
            pltpu.VMEM((2 * heads * (positions // 8), block, block), F32),
            pltpu.VMEM((2 * half, count), F32),
            dma((7,)),
        ],
        flops=12 * count * half * width,
        nbytes=10_000_000,
        mib=63.1,
    )(moved, temporal_in, temporal_in_other)
    returned = lax.all_to_all(attended, "seq", 0, 0, tiled=True)
    tiles = width // LANES
    out = call(
        final_kernel,
        shape((count * tiles, LANES), F32),
        [HBM] * 4 + [VMEM],
        [
            pltpu.VMEM(tokens_shape, BF16),
            pltpu.VMEM((2 * half, width), BF16),
            pltpu.VMEM((count, width), F32),
            pltpu.VMEM((count * tiles, LANES), F32),
            dma((4 + CHUNKS,)),
        ],
        flops=4 * count * half * width,
        nbytes=8_000_000,
        out_specs=HBM,
        mib=63.1,
    )(returned, temporal_out, temporal_out_other, middle, temporal_mods)
    return out.reshape(frames.shape)


def solution(mesh):
    return jax.shard_map(
        body,
        mesh=mesh,
        in_specs=(
            P("tp", ("clip", "seq"), None),
            P("clip"),
            P(),
            P(("seq", "tp"), None),
            P(),
            P(),
            P(None, None, "tp"),
            P("tp", None),
            P(None, None, "tp"),
            P("tp", None),
        ),
        out_specs=P("tp", ("clip", "seq"), None),
        check_vma=False,
    )
```

```python
import functools
import math

import jax
import jax.numpy as jnp
from jax import lax
from jax.experimental import pallas as pl
from jax.experimental.pallas import tpu as pltpu
from jax.sharding import PartitionSpec as P

HEAD_DIM = 72
FREQ = 256
LANES = 128
SWAP = [(0, 1), (1, 0)]
VMEM = pl.BlockSpec(memory_space=pltpu.VMEM)
HBM = pl.BlockSpec(memory_space=pl.ANY)
TERM_ROWS = 32
CHUNKS = 4
SCALE = math.log2(math.e) / math.sqrt(HEAD_DIM)
BF16 = jnp.bfloat16
F32 = jnp.float32


def call(kernel, outs, in_specs, scratch=(), flops=0, nbytes=0, out_specs=None, mib=63.1):
    return pl.pallas_call(
        kernel,
        out_shape=outs,
        in_specs=in_specs,
        out_specs=out_specs or jax.tree.map(lambda _: VMEM, outs),
        scratch_shapes=list(scratch),
        compiler_params=pltpu.CompilerParams(vmem_limit_bytes=int(mib * 1024 * 1024)),
        cost_estimate=pl.CostEstimate(flops=flops, bytes_accessed=nbytes, transcendentals=0),
    )


def dot_nt(a, b):
    return lax.dot_general(a, b, (((1,), (1,)), ((), ())), preferred_element_type=F32)


def normalise(tokens, shift, scale):
    mean = jnp.mean(tokens, axis=-1, keepdims=True)
    centred = tokens - mean
    variance = jnp.mean(centred * centred, axis=-1, keepdims=True)
    return (centred * lax.rsqrt(variance + 1e-06) * (1.0 + scale) + shift).astype(BF16)


def fetch(source, target, sem):
    copy = pltpu.make_async_copy(source, target, sem)
    copy.start()
    return copy


def window(head):
    first = head * HEAD_DIM // LANES * LANES
    last = -(-(head + 1) * HEAD_DIM // LANES) * LANES
    return first, last


def padded(width):
    return -(-width // LANES) * LANES


def head_queries(queries, head):
    first, last = window(head)
    start = head * HEAD_DIM
    pieces = [queries[start : start + HEAD_DIM]]
    tokens = queries.shape[1]
    if start > first:
        pieces.insert(0, jnp.zeros((start - first, tokens), F32))
    if last > start + HEAD_DIM:
        pieces.append(jnp.zeros((last - start - HEAD_DIM, tokens), F32))
    return jnp.concatenate(pieces, axis=0).astype(BF16)


def head_values(values, head):
    start = head * HEAD_DIM
    ones = jnp.ones((8, values.shape[1]), F32)
    return jnp.concatenate([values[start : start + HEAD_DIM], ones], axis=0).astype(BF16)


def head_scores(queries, keys, head):
    first, last = window(head)
    return jnp.dot(keys[:, first:last], head_queries(queries, head), preferred_element_type=F32)


def head_output(scores, values):
    peak = jnp.max(scores, axis=0, keepdims=True)
    raised = jnp.exp2((scores - peak) * SCALE).astype(BF16)
    out = jnp.dot(values, raised, preferred_element_type=F32)
    return out[:HEAD_DIM] / out[HEAD_DIM : HEAD_DIM + 1]


def modulation_table(total, table):
    tiles = table.shape[1] // LANES
    rows = []
    for row in range(3):
        parts = [total[row * tiles + t : row * tiles + t + 1] for t in range(tiles)]
        rows.append(jnp.concatenate(parts, axis=1))
    return jnp.concatenate(rows, axis=0)


def fetch_parts(w_hbm, w, sems):
    half = w.shape[1]
    return [fetch(w_hbm.at[pl.ds(p * half, half)], w.at[p], sems.at[p]) for p in range(3)]


def spatial_kernel(
    heads,
    tok_hbm,
    far_hbm,
    own_total,
    other_total,
    table,
    next_table,
    w_hbm,
    after,
    mods_out,
    next_out,
    normed_out,
    k_out,
    v_out,
    att_out,
    tok,
    far,
    w,
    q,
    k,
    v,
    scores,
    sems,
):
    count, half = far.shape[0], heads * HEAD_DIM
    in_far = fetch(far_hbm, far, sems.at[4])
    in_w = fetch_parts(w_hbm, w, sems)
    in_tok = fetch(tok_hbm, tok, sems.at[5])
    near, beyond = pl.ds(0, count), pl.ds(count, count)
    k[:, k.shape[1] - LANES :] = jnp.zeros((2 * count, LANES), BF16)
    modulation = modulation_table(own_total[...] + other_total[...], table)
    mods = table[...] + modulation
    mods_out[...] = mods
    next_out[...] = next_table[...] + modulation
    in_far.wait()
    normed_far = normalise(far[...].astype(F32), mods[0:1], mods[1:2])
    in_w[0].wait()
    q[...] = dot_nt(w[0], normed_far)
    in_w[1].wait()
    k[beyond, :half] = dot_nt(normed_far, w[1]).astype(BF16)
    in_tok.wait()
    normed = normalise(tok[...].astype(F32), mods[0:1], mods[1:2])
    tok[...] = normed
    out_normed = fetch(tok, normed_out, sems.at[8])
    k[near, :half] = dot_nt(normed, w[1]).astype(BF16)
    out_k = fetch(k, k_out, sems.at[6])
    for head in range(heads):
        scores[head] = head_scores(q, k, head)
    in_w[2].wait()
    values = dot_nt(w[2], normed)
    for head in range(heads):
        v[head, :, :count] = head_values(values, head)
    values = dot_nt(w[2], normed_far)
    for head in range(heads):
        v[head, :, count:] = head_values(values, head)
    out_v = fetch(v, v_out, sems.at[7])
    outs = [head_output(scores[head], v[head]) for head in range(heads)]
    att_out[...] = jnp.concatenate(outs, axis=0).T.astype(BF16)
    for copy in (out_k, out_v, out_normed):
        copy.wait()


def near_kernel(
    heads,
    normed_hbm,
    in_w_hbm,
    k_hbm,
    v_hbm,
    tok_hbm,
    mods,
    w_hbm,
    part_out,
    normed,
    in_w,
    k,
    v,
    tok,
    w,
    scores,
    sems,
):
    half = heads * HEAD_DIM
    copies = [
        fetch(normed_hbm, normed, sems.at[0]),
        fetch(in_w_hbm.at[pl.ds(0, half)], in_w, sems.at[1]),
        fetch(k_hbm, k, sems.at[2]),
        fetch(v_hbm, v, sems.at[3]),
        fetch(w_hbm, w, sems.at[4]),
        fetch(tok_hbm, tok, sems.at[5]),
    ]
    copies[0].wait()
    copies[1].wait()
    queries = dot_nt(in_w[...], normed[...])
    copies[2].wait()
    for head in range(heads):
        scores[head] = head_scores(queries, k, head)
    copies[3].wait()
    outs = [head_output(scores[head], v[head]) for head in range(heads)]
    attended = jnp.concatenate(outs, axis=0).T.astype(BF16)
    copies[4].wait()
    projected = jnp.dot(attended, w[...], preferred_element_type=F32)
    copies[5].wait()
    part_out[...] = tok[...].astype(F32) + mods[2:3] * projected


def piece_kernel(own_hbm, after, out_hbm, piece, sems):
    fetch(own_hbm, piece, sems.at[0]).wait()
    fetch(piece, out_hbm, sems.at[1]).wait()


def middle_kernel(
    part_hbm,
    att_hbm,
    w_hbm,
    mods,
    next_mods,
    middle_hbm,
    normed_hbm,
    part,
    att,
    w,
    middle,
    normed,
    sems,
):
    in_w = fetch(w_hbm, w, sems.at[0])
    in_att = fetch(att_hbm, att, sems.at[3])
    in_part = fetch(part_hbm, part, sems.at[1])
    in_w.wait()
    in_att.wait()
    projected = jnp.dot(att[...], w[...], preferred_element_type=F32)
    in_part.wait()
    half = middle.shape[0] // 2
    copies = []
    for side in range(2):
        rows = pl.ds(side * half, half)
        values = part[rows, :] + mods[2:3] * projected[side * half : (side + 1) * half]
        middle[rows, :] = values
        normed[rows, :] = normalise(values, next_mods[0:1], next_mods[1:2])
        copies.append(fetch(normed.at[rows], normed_hbm.at[rows], sems.at[4 + 2 * side]))
        copies.append(fetch(middle.at[rows], middle_hbm.at[rows], sems.at[5 + 2 * side]))
    for copy in copies:
        copy.wait()


def temporal_kernel(
    heads, positions, moved_hbm, own_hbm, other_hbm, att_out, moved, w, k, scores, out, sems
):
    half = heads * HEAD_DIM
    in_moved = fetch(moved_hbm, moved, sems.at[6])
    count, width = moved.shape
    depth = count // positions
    groups = positions // 8
    block = depth * 8
    copies = []
    for part in range(3):
        for side, source in enumerate((own_hbm, other_hbm)):
            rows = pl.ds(side * half, half)
            copies.append(
                fetch(
                    source.at[pl.ds(part * half, half)],
                    w.at[part, rows],
                    sems.at[part * 2 + side],
                )
            )
    here = lax.rem(lax.broadcasted_iota(jnp.int32, (block, block), 0), 8)
    there = lax.rem(lax.broadcasted_iota(jnp.int32, (block, block), 1), 8)
    bias = jnp.where(here == there, 0.0, -1e30)
    in_moved.wait()
    grid = moved[...].astype(F32).reshape(depth, positions, width)
    tokens = jnp.concatenate(
        [grid[:, g * 8 : g * 8 + 8].reshape(block, width) for g in range(groups)], axis=0
    ).astype(BF16)
    copies[0].wait()
    copies[1].wait()
    queries = dot_nt(w[0], tokens)
    copies[2].wait()
    copies[3].wait()
    k[...] = dot_nt(tokens, w[1]).astype(BF16)
    spans = [slice(g * block, (g + 1) * block) for g in range(groups)]
    for head in range(2 * heads):
        first, last = window(head)
        head_q = head_queries(queries, head)
        for g, span in enumerate(spans):
            scores[head * groups + g] = (
                jnp.dot(k[span, first:last], head_q[:, span], preferred_element_type=F32) + bias
            )
    copies[4].wait()
    copies[5].wait()
    values = dot_nt(w[2], tokens)
    for head in range(2 * heads):
        head_v = head_values(values, head)
        outs = [
            head_output(scores[head * groups + g], head_v[:, span])
            for g, span in enumerate(spans)
        ]
        out[pl.ds(head * HEAD_DIM, HEAD_DIM), :] = jnp.concatenate(outs, axis=1)
    result = out[...].T
    by_group = [result[span].reshape(depth, 8, 2 * half) for span in spans]
    att_out[...] = jnp.concatenate(by_group, axis=1).reshape(count, 2 * half).astype(BF16)


def final_kernel(
    att_hbm, own_w, other_w, middle_hbm, mods, out_hbm, att, w, middle, out, sems
):
    half = own_w.shape[0]
    in_att = fetch(att_hbm, att, sems.at[3 + CHUNKS])
    copies = [
        fetch(own_w, w.at[pl.ds(0, half)], sems.at[0]),
        fetch(other_w, w.at[pl.ds(half, half)], sems.at[1]),
        fetch(middle_hbm, middle, sems.at[2]),
    ]
    count, width = middle.shape
    tiles = width // LANES
    chunk = count // CHUNKS
    split = half // LANES * LANES
    in_att.wait()
    copies[0].wait()
    early = jnp.dot(att[:, :split], w[:split, :], preferred_element_type=F32)
    copies[1].wait()
    stores = []
    for part in range(CHUNKS):
        rows = pl.ds(part * chunk, chunk)
        projected = early[part * chunk : (part + 1) * chunk]
        projected += jnp.dot(att[rows, split:], w[split:, :], preferred_element_type=F32)
        if part == 0:
            copies[2].wait()
        result = middle[rows, :] + mods[2:3] * projected
        base = part * chunk * tiles
        for tile in range(tiles):
            out[pl.ds(base + tile, chunk, tiles), :] = result[
                :, tile * LANES : (tile + 1) * LANES
            ]
        span = pl.ds(base, chunk * tiles)
        stores.append(fetch(out.at[span], out_hbm.at[span], sems.at[3 + part]))
    for store in stores:
        store.wait()


def time_features(timestep):
    half = FREQ // 2
    ladder = jnp.exp(-math.log(10000.0) * jnp.arange(half, dtype=F32) / half)
    angles = timestep.astype(F32)[:, None] * ladder[None, :]
    return jnp.concatenate([jnp.cos(angles), jnp.sin(angles)], axis=-1)


def modulation_terms(timestep, embed_weight, block_weight):
    features = time_features(timestep)
    embedded = jax.nn.silu(
        jnp.dot(features, embed_weight.astype(F32), precision=lax.Precision.HIGHEST)
    )
    count, width = block_weight.shape
    start = lax.axis_index(("seq", "tp")) * count
    mine = lax.dynamic_slice_in_dim(embedded, start, count, 1)
    term = jnp.dot(mine, block_weight.astype(F32), precision=lax.Precision.HIGHEST)
    tiles = width // LANES
    return jnp.pad(term.reshape(tiles, LANES), ((0, TERM_ROWS - tiles), (0, 0)))


def eighth(weight):
    rows = weight.shape[0] // lax.axis_size("clip")
    return lax.dynamic_slice_in_dim(weight, lax.axis_index("clip") * rows, rows, 0)


def body(
    frames,
    timestep,
    embed_weight,
    block_weight,
    spatial_table,
    temporal_table,
    spatial_qkv,
    spatial_out,
    temporal_qkv,
    temporal_out,
):
    width = frames.shape[-1]
    tokens = frames.reshape(-1, width)
    count = tokens.shape[0]
    half = spatial_out.shape[0]
    heads = half // HEAD_DIM
    far = lax.ppermute(tokens, "tp", SWAP)
    spatial_in = jnp.transpose(spatial_qkv, (1, 2, 0)).reshape(-1, width)
    temporal_in = jnp.transpose(temporal_qkv, (1, 2, 0)).reshape(-1, width)

    shape = jax.ShapeDtypeStruct
    dma = pltpu.SemaphoreType.DMA
    group = lax.axis_size("seq") * lax.axis_size("tp")
    across = [(i, i ^ 3) for i in range(group)]
    out_piece = lax.ppermute(eighth(spatial_out), ("seq", "tp"), across)
    term = modulation_terms(timestep, embed_weight, block_weight)
    copies = jnp.broadcast_to(term[None], (lax.axis_size("seq"),) + term.shape)
    terms = lax.all_to_all(copies.reshape(-1, LANES), "seq", 0, 0, tiled=True)
    own_total = jnp.sum(terms.reshape(copies.shape), axis=0)
    other_total = lax.ppermute(own_total, "tp", SWAP)
    own_piece = eighth(temporal_in)
    own_piece = call(
        piece_kernel,
        shape(own_piece.shape, BF16),
        [HBM] * 2,
        [pltpu.VMEM(own_piece.shape, BF16), dma((2,))],
        flops=20_000_000_000,
        nbytes=1_500_000,
        out_specs=HBM,
    )(own_piece, far)
    out_piece, _ = lax.optimization_barrier((out_piece, (own_total, far)))
    spatial_out_other = lax.all_gather(out_piece, "clip", axis=0, tiled=True)
    piece = lax.ppermute(own_piece, ("seq", "tp"), across)

    tokens_shape = (count, width)
    k_shape = (2 * count, padded(half))
    v_shape = (heads, HEAD_DIM + 8, 2 * count)
    all_scores = pltpu.VMEM((heads, 2 * count, count), F32)
    spatial_mods, temporal_mods, normed, k, v, far_attended = call(
        functools.partial(spatial_kernel, heads),
        (
            shape((3, width), F32),
            shape((3, width), F32),
            shape(tokens_shape, BF16),
            shape(k_shape, BF16),
            shape(v_shape, BF16),
            shape((count, half), BF16),
        ),
        [HBM] * 2 + [VMEM] * 4 + [HBM] * 2,
        [
            pltpu.VMEM(tokens_shape, BF16),
            pltpu.VMEM(tokens_shape, BF16),
            pltpu.VMEM((3, half, width), BF16),
            pltpu.VMEM((half, count), F32),
            pltpu.VMEM(k_shape, BF16),
            pltpu.VMEM(v_shape, BF16),
            all_scores,
            dma((9,)),
        ],
        flops=14 * count * half * width,
        nbytes=14_000_000,
        out_specs=(VMEM, VMEM, HBM, HBM, HBM, VMEM),
        mib=63.1,
    )(tokens, far, own_total, other_total, spatial_table, temporal_table, spatial_in, own_piece)
    attended = lax.ppermute(far_attended, "tp", SWAP)
    part = call(
        functools.partial(near_kernel, heads),
        shape(tokens_shape, F32),
        [HBM] * 5 + [VMEM, HBM],
        [
            pltpu.VMEM(tokens_shape, BF16),
            pltpu.VMEM((half, width), BF16),
            pltpu.VMEM(k_shape, BF16),
            pltpu.VMEM(v_shape, BF16),
            pltpu.VMEM(tokens_shape, BF16),
            pltpu.VMEM((half, width), BF16),
            all_scores,
            dma((6,)),
        ],
        flops=6 * count * half * width,
        nbytes=8_000_000,
        mib=63.1,
    )(normed, spatial_in, k, v, tokens, spatial_mods, spatial_out)
    piece, _ = lax.optimization_barrier((piece, (attended, part)))
    temporal_in_other = lax.all_gather(piece, "clip", axis=0, tiled=True)
    middle, normed = call(
        middle_kernel,
        (shape(tokens_shape, F32), shape(tokens_shape, BF16)),
        [HBM] * 3 + [VMEM] * 2,
        [
            pltpu.VMEM(tokens_shape, F32),
            pltpu.VMEM((count, half), BF16),
            pltpu.VMEM((half, width), BF16),
            pltpu.VMEM(tokens_shape, F32),
            pltpu.VMEM(tokens_shape, BF16),
            dma((8,)),
        ],
        flops=2 * count * half * width,
        nbytes=6_000_000,
        out_specs=(HBM, HBM),
        mib=63.1,
    )(part, attended, spatial_out_other, spatial_mods, temporal_mods)

    out_piece, _ = lax.optimization_barrier((eighth(temporal_out), normed))
    out_piece = lax.ppermute(out_piece, ("seq", "tp"), across)
    temporal_out_other = lax.all_gather(out_piece, "clip", axis=0, tiled=True)
    moved = lax.all_to_all(normed, "seq", 0, 0, tiled=True)
    positions = count // lax.axis_size("seq")
    block = 8 * lax.axis_size("seq")
    attended = call(
        functools.partial(temporal_kernel, heads, positions),
        shape((count, 2 * half), BF16),
        [HBM] * 3,
        [
            pltpu.VMEM(tokens_shape, BF16),
            pltpu.VMEM((3, 2 * half, width), BF16),
            pltpu.VMEM((count, 2 * half), BF16),
            pltpu.VMEM((2 * heads * (positions // 8), block, block), F32),
            pltpu.VMEM((2 * half, count), F32),
            dma((7,)),
        ],
        flops=12 * count * half * width,
        nbytes=10_000_000,
        mib=63.1,
    )(moved, temporal_in, temporal_in_other)
    returned = lax.all_to_all(attended, "seq", 0, 0, tiled=True)
    tiles = width // LANES
    out = call(
        final_kernel,
        shape((count * tiles, LANES), F32),
        [HBM] * 4 + [VMEM],
        [
            pltpu.VMEM(tokens_shape, BF16),
            pltpu.VMEM((2 * half, width), BF16),
            pltpu.VMEM((count, width), F32),
            pltpu.VMEM((count * tiles, LANES), F32),
            dma((4 + CHUNKS,)),
        ],
        flops=4 * count * half * width,
        nbytes=8_000_000,
        out_specs=HBM,
        mib=63.1,
    )(returned, temporal_out, temporal_out_other, middle, temporal_mods)
    return out.reshape(frames.shape)


def solution(mesh):
    return jax.shard_map(
        body,
        mesh=mesh,
        in_specs=(
            P("tp", ("clip", "seq"), None),
            P("clip"),
            P(),
            P(("seq", "tp"), None),
            P(),
            P(),
            P(None, None, "tp"),
            P("tp", None),
            P(None, None, "tp"),
            P("tp", None),
        ),
        out_specs=P("tp", ("clip", "seq"), None),
        check_vma=False,
    )
```

```python
import functools
import math

import jax
import jax.numpy as jnp
from jax import lax
from jax.experimental import pallas as pl
from jax.experimental.pallas import tpu as pltpu
from jax.sharding import PartitionSpec as P

HEAD_DIM = 72
FREQ = 256
LANES = 128
SWAP = [(0, 1), (1, 0)]
VMEM = pl.BlockSpec(memory_space=pltpu.VMEM)
HBM = pl.BlockSpec(memory_space=pl.ANY)
TERM_ROWS = 32
CHUNKS = 4
SCALE = math.log2(math.e) / math.sqrt(HEAD_DIM)
BF16 = jnp.bfloat16
F32 = jnp.float32


def call(kernel, outs, in_specs, scratch=(), flops=0, nbytes=0, out_specs=None, mib=63.1):
    return pl.pallas_call(
        kernel,
        out_shape=outs,
        in_specs=in_specs,
        out_specs=out_specs or jax.tree.map(lambda _: VMEM, outs),
        scratch_shapes=list(scratch),
        compiler_params=pltpu.CompilerParams(vmem_limit_bytes=int(mib * 1024 * 1024)),
        cost_estimate=pl.CostEstimate(flops=flops, bytes_accessed=nbytes, transcendentals=0),
    )


def dot_nt(a, b):
    return lax.dot_general(a, b, (((1,), (1,)), ((), ())), preferred_element_type=F32)


def normalise(tokens, shift, scale):
    mean = jnp.mean(tokens, axis=-1, keepdims=True)
    centred = tokens - mean
    variance = jnp.mean(centred * centred, axis=-1, keepdims=True)
    return (centred * lax.rsqrt(variance + 1e-06) * (1.0 + scale) + shift).astype(BF16)


def fetch(source, target, sem):
    copy = pltpu.make_async_copy(source, target, sem)
    copy.start()
    return copy


def window(head):
    first = head * HEAD_DIM // LANES * LANES
    last = -(-(head + 1) * HEAD_DIM // LANES) * LANES
    return first, last


def padded(width):
    return -(-width // LANES) * LANES


def head_queries(queries, head):
    first, last = window(head)
    start = head * HEAD_DIM
    pieces = [queries[start : start + HEAD_DIM]]
    tokens = queries.shape[1]
    if start > first:
        pieces.insert(0, jnp.zeros((start - first, tokens), F32))
    if last > start + HEAD_DIM:
        pieces.append(jnp.zeros((last - start - HEAD_DIM, tokens), F32))
    return jnp.concatenate(pieces, axis=0).astype(BF16)


def head_values(values, head):
    start = head * HEAD_DIM
    ones = jnp.ones((8, values.shape[1]), F32)
    return jnp.concatenate([values[start : start + HEAD_DIM], ones], axis=0).astype(BF16)


def head_scores(queries, keys, head):
    first, last = window(head)
    return jnp.dot(keys[:, first:last], head_queries(queries, head), preferred_element_type=F32)


def head_output(scores, values):
    peak = jnp.max(scores, axis=0, keepdims=True)
    raised = jnp.exp2(scores - peak).astype(BF16)
    out = jnp.dot(values, raised, preferred_element_type=F32)
    return out[:HEAD_DIM] / out[HEAD_DIM : HEAD_DIM + 1]


def modulation_table(total, table):
    tiles = table.shape[1] // LANES
    rows = []
    for row in range(3):
        parts = [total[row * tiles + t : row * tiles + t + 1] for t in range(tiles)]
        rows.append(jnp.concatenate(parts, axis=1))
    return jnp.concatenate(rows, axis=0)


def fetch_parts(w_hbm, w, sems):
    half = w.shape[1]
    return [fetch(w_hbm.at[pl.ds(p * half, half)], w.at[p], sems.at[p]) for p in range(3)]


def spatial_kernel(
    heads,
    tok_hbm,
    far_hbm,
    own_total,
    other_total,
    table,
    next_table,
    w_hbm,
    mods_out,
    next_out,
    normed_out,
    k_out,
    v_out,
    att_out,
    tok,
    far,
    w,
    q,
    k,
    v,
    scores,
    sems,
):
    count, half = far.shape[0], heads * HEAD_DIM
    in_far = fetch(far_hbm, far, sems.at[4])
    in_w = fetch_parts(w_hbm, w, sems)
    in_tok = fetch(tok_hbm, tok, sems.at[5])
    near, beyond = pl.ds(0, count), pl.ds(count, count)
    k[:, k.shape[1] - LANES :] = jnp.zeros((2 * count, LANES), BF16)
    modulation = modulation_table(own_total[...] + other_total[...], table)
    mods = table[...] + modulation
    mods_out[...] = mods
    next_out[...] = next_table[...] + modulation
    in_far.wait()
    normed_far = normalise(far[...].astype(F32), mods[0:1], mods[1:2])
    in_w[0].wait()
    q[...] = dot_nt(w[0], normed_far) * SCALE
    in_w[1].wait()
    k[beyond, :half] = dot_nt(normed_far, w[1]).astype(BF16)
    in_tok.wait()
    normed = normalise(tok[...].astype(F32), mods[0:1], mods[1:2])
    tok[...] = normed
    out_normed = fetch(tok, normed_out, sems.at[8])
    k[near, :half] = dot_nt(normed, w[1]).astype(BF16)
    out_k = fetch(k, k_out, sems.at[6])
    for head in range(heads):
        scores[head] = head_scores(q, k, head)
    in_w[2].wait()
    values = dot_nt(w[2], normed)
    for head in range(heads):
        v[head, :, :count] = head_values(values, head)
    values = dot_nt(w[2], normed_far)
    for head in range(heads):
        v[head, :, count:] = head_values(values, head)
    out_v = fetch(v, v_out, sems.at[7])
    outs = [head_output(scores[head], v[head]) for head in range(heads)]
    att_out[...] = jnp.concatenate(outs, axis=0).T.astype(BF16)
    for copy in (out_k, out_v, out_normed):
        copy.wait()


def near_kernel(
    heads,
    normed_hbm,
    in_w_hbm,
    k_hbm,
    v_hbm,
    tok_hbm,
    mods,
    w_hbm,
    part_out,
    normed,
    in_w,
    k,
    v,
    tok,
    w,
    scores,
    sems,
):
    half = heads * HEAD_DIM
    copies = [
        fetch(normed_hbm, normed, sems.at[0]),
        fetch(in_w_hbm.at[pl.ds(0, half)], in_w, sems.at[1]),
        fetch(k_hbm, k, sems.at[2]),
        fetch(v_hbm, v, sems.at[3]),
        fetch(w_hbm, w, sems.at[4]),
        fetch(tok_hbm, tok, sems.at[5]),
    ]
    copies[0].wait()
    copies[1].wait()
    queries = dot_nt(in_w[...], normed[...]) * SCALE
    copies[2].wait()
    for head in range(heads):
        scores[head] = head_scores(queries, k, head)
    copies[3].wait()
    outs = [head_output(scores[head], v[head]) for head in range(heads)]
    attended = jnp.concatenate(outs, axis=0).T.astype(BF16)
    copies[4].wait()
    projected = jnp.dot(attended, w[...], preferred_element_type=F32)
    copies[5].wait()
    part_out[...] = tok[...].astype(F32) + mods[2:3] * projected


def middle_kernel(
    part_hbm, att_hbm, w_hbm, mods, next_mods, middle_hbm, normed_out, part, att, w, middle, sems
):
    in_w = fetch(w_hbm, w, sems.at[0])
    in_att = fetch(att_hbm, att, sems.at[3])
    in_part = fetch(part_hbm, part, sems.at[1])
    in_w.wait()
    in_att.wait()
    projected = jnp.dot(att[...], w[...], preferred_element_type=F32)
    in_part.wait()
    middle[...] = part[...] + mods[2:3] * projected
    copy = fetch(middle, middle_hbm, sems.at[2])
    normed_out[...] = normalise(middle[...], next_mods[0:1], next_mods[1:2])
    copy.wait()


def temporal_kernel(
    heads, positions, moved_hbm, own_hbm, other_hbm, att_out, moved, w, k, scores, out, sems
):
    half = heads * HEAD_DIM
    in_moved = fetch(moved_hbm, moved, sems.at[6])
    count, width = moved.shape
    depth = count // positions
    groups = positions // 8
    block = depth * 8
    copies = []
    for part in range(3):
        for side, source in enumerate((own_hbm, other_hbm)):
            rows = pl.ds(side * half, half)
            copies.append(
                fetch(
                    source.at[pl.ds(part * half, half)],
                    w.at[part, rows],
                    sems.at[part * 2 + side],
                )
            )
    here = lax.rem(lax.broadcasted_iota(jnp.int32, (block, block), 0), 8)
    there = lax.rem(lax.broadcasted_iota(jnp.int32, (block, block), 1), 8)
    bias = jnp.where(here == there, 0.0, -1e30)
    in_moved.wait()
    grid = moved[...].astype(F32).reshape(depth, positions, width)
    tokens = jnp.concatenate(
        [grid[:, g * 8 : g * 8 + 8].reshape(block, width) for g in range(groups)], axis=0
    ).astype(BF16)
    copies[0].wait()
    copies[1].wait()
    queries = dot_nt(w[0], tokens) * SCALE
    copies[2].wait()
    copies[3].wait()
    k[...] = dot_nt(tokens, w[1]).astype(BF16)
    spans = [slice(g * block, (g + 1) * block) for g in range(groups)]
    for head in range(2 * heads):
        first, last = window(head)
        head_q = head_queries(queries, head)
        for g, span in enumerate(spans):
            scores[head * groups + g] = (
                jnp.dot(k[span, first:last], head_q[:, span], preferred_element_type=F32) + bias
            )
    copies[4].wait()
    copies[5].wait()
    values = dot_nt(w[2], tokens)
    for head in range(2 * heads):
        head_v = head_values(values, head)
        outs = [
            head_output(scores[head * groups + g], head_v[:, span])
            for g, span in enumerate(spans)
        ]
        out[pl.ds(head * HEAD_DIM, HEAD_DIM), :] = jnp.concatenate(outs, axis=1)
    result = out[...].T
    by_group = [result[span].reshape(depth, 8, 2 * half) for span in spans]
    att_out[...] = jnp.concatenate(by_group, axis=1).reshape(count, 2 * half).astype(BF16)


def final_kernel(
    att_hbm, own_w, other_w, middle_hbm, mods, out_hbm, att, w, middle, out, sems
):
    half = own_w.shape[0]
    in_att = fetch(att_hbm, att, sems.at[3 + CHUNKS])
    copies = [
        fetch(own_w, w.at[pl.ds(0, half)], sems.at[0]),
        fetch(other_w, w.at[pl.ds(half, half)], sems.at[1]),
        fetch(middle_hbm, middle, sems.at[2]),
    ]
    count, width = middle.shape
    tiles = width // LANES
    chunk = count // CHUNKS
    split = half // LANES * LANES
    in_att.wait()
    copies[0].wait()
    early = jnp.dot(att[:, :split], w[:split, :], preferred_element_type=F32)
    copies[1].wait()
    stores = []
    for part in range(CHUNKS):
        rows = pl.ds(part * chunk, chunk)
        projected = early[part * chunk : (part + 1) * chunk]
        projected += jnp.dot(att[rows, split:], w[split:, :], preferred_element_type=F32)
        if part == 0:
            copies[2].wait()
        result = middle[rows, :] + mods[2:3] * projected
        base = part * chunk * tiles
        for tile in range(tiles):
            out[pl.ds(base + tile, chunk, tiles), :] = result[
                :, tile * LANES : (tile + 1) * LANES
            ]
        span = pl.ds(base, chunk * tiles)
        stores.append(fetch(out.at[span], out_hbm.at[span], sems.at[3 + part]))
    for store in stores:
        store.wait()


def time_features(timestep):
    half = FREQ // 2
    ladder = jnp.exp(-math.log(10000.0) * jnp.arange(half, dtype=F32) / half)
    angles = timestep.astype(F32)[:, None] * ladder[None, :]
    return jnp.concatenate([jnp.cos(angles), jnp.sin(angles)], axis=-1)


def modulation_terms(timestep, embed_weight, block_weight):
    features = time_features(timestep)
    embedded = jax.nn.silu(
        jnp.dot(features, embed_weight.astype(F32), precision=lax.Precision.HIGHEST)
    )
    count, width = block_weight.shape
    start = lax.axis_index(("seq", "tp")) * count
    mine = lax.dynamic_slice_in_dim(embedded, start, count, 1)
    term = jnp.dot(mine, block_weight.astype(F32), precision=lax.Precision.HIGHEST)
    tiles = width // LANES
    return jnp.pad(term.reshape(tiles, LANES), ((0, TERM_ROWS - tiles), (0, 0)))


def eighth(weight):
    rows = weight.shape[0] // lax.axis_size("clip")
    return lax.dynamic_slice_in_dim(weight, lax.axis_index("clip") * rows, rows, 0)


def body(
    frames,
    timestep,
    embed_weight,
    block_weight,
    spatial_table,
    temporal_table,
    spatial_qkv,
    spatial_out,
    temporal_qkv,
    temporal_out,
):
    width = frames.shape[-1]
    tokens = frames.reshape(-1, width)
    count = tokens.shape[0]
    half = spatial_out.shape[0]
    heads = half // HEAD_DIM
    far = lax.ppermute(tokens, "tp", SWAP)
    spatial_in = jnp.transpose(spatial_qkv, (1, 2, 0)).reshape(-1, width)
    temporal_in = jnp.transpose(temporal_qkv, (1, 2, 0)).reshape(-1, width)

    shape = jax.ShapeDtypeStruct
    dma = pltpu.SemaphoreType.DMA
    group = lax.axis_size("seq") * lax.axis_size("tp")
    across = [(i, i ^ 3) for i in range(group)]
    out_piece = lax.ppermute(eighth(spatial_out), ("seq", "tp"), across)
    term = modulation_terms(timestep, embed_weight, block_weight)
    copies = jnp.broadcast_to(term[None], (lax.axis_size("seq"),) + term.shape)
    terms = lax.all_to_all(copies.reshape(-1, LANES), "seq", 0, 0, tiled=True)
    own_total = jnp.sum(terms.reshape(copies.shape), axis=0)
    other_total = lax.ppermute(own_total, "tp", SWAP)
    own_piece = eighth(temporal_in)
    own_piece, _ = lax.optimization_barrier((own_piece, far))
    out_piece, _ = lax.optimization_barrier((out_piece, (own_total, far)))
    spatial_out_other = lax.all_gather(out_piece, "clip", axis=0, tiled=True)
    piece = lax.ppermute(own_piece, ("seq", "tp"), across)

    tokens_shape = (count, width)
    k_shape = (2 * count, padded(half))
    v_shape = (heads, HEAD_DIM + 8, 2 * count)
    all_scores = pltpu.VMEM((heads, 2 * count, count), F32)
    spatial_mods, temporal_mods, normed, k, v, far_attended = call(
        functools.partial(spatial_kernel, heads),
        (
            shape((3, width), F32),
            shape((3, width), F32),
            shape(tokens_shape, BF16),
            shape(k_shape, BF16),
            shape(v_shape, BF16),
            shape((count, half), BF16),
        ),
        [HBM] * 2 + [VMEM] * 4 + [HBM],
        [
            pltpu.VMEM(tokens_shape, BF16),
            pltpu.VMEM(tokens_shape, BF16),
            pltpu.VMEM((3, half, width), BF16),
            pltpu.VMEM((half, count), F32),
            pltpu.VMEM(k_shape, BF16),
            pltpu.VMEM(v_shape, BF16),
            all_scores,
            dma((9,)),
        ],
        flops=14 * count * half * width,
        nbytes=14_000_000,
        out_specs=(VMEM, VMEM, HBM, HBM, HBM, VMEM),
        mib=63.1,
    )(tokens, far, own_total, other_total, spatial_table, temporal_table, spatial_in)
    attended = lax.ppermute(far_attended, "tp", SWAP)
    part = call(
        functools.partial(near_kernel, heads),
        shape(tokens_shape, F32),
        [HBM] * 5 + [VMEM, HBM],
        [
            pltpu.VMEM(tokens_shape, BF16),
            pltpu.VMEM((half, width), BF16),
            pltpu.VMEM(k_shape, BF16),
            pltpu.VMEM(v_shape, BF16),
            pltpu.VMEM(tokens_shape, BF16),
            pltpu.VMEM((half, width), BF16),
            all_scores,
            dma((6,)),
        ],
        flops=6 * count * half * width,
        nbytes=8_000_000,
        mib=63.1,
    )(normed, spatial_in, k, v, tokens, spatial_mods, spatial_out)
    piece, _ = lax.optimization_barrier((piece, (attended, part)))
    temporal_in_other = lax.all_gather(piece, "clip", axis=0, tiled=True)
    middle, normed = call(
        middle_kernel,
        (shape(tokens_shape, F32), shape(tokens_shape, BF16)),
        [HBM] * 3 + [VMEM] * 2,
        [
            pltpu.VMEM(tokens_shape, F32),
            pltpu.VMEM((count, half), BF16),
            pltpu.VMEM((half, width), BF16),
            pltpu.VMEM(tokens_shape, F32),
            dma((4,)),
        ],
        flops=2 * count * half * width,
        nbytes=6_000_000,
        out_specs=(HBM, VMEM),
        mib=63.1,
    )(part, attended, spatial_out_other, spatial_mods, temporal_mods)

    out_piece, _ = lax.optimization_barrier((eighth(temporal_out), normed))
    out_piece = lax.ppermute(out_piece, ("seq", "tp"), across)
    temporal_out_other = lax.all_gather(out_piece, "clip", axis=0, tiled=True)
    moved = lax.all_to_all(normed, "seq", 0, 0, tiled=True)
    positions = count // lax.axis_size("seq")
    block = 8 * lax.axis_size("seq")
    attended = call(
        functools.partial(temporal_kernel, heads, positions),
        shape((count, 2 * half), BF16),
        [HBM] * 3,
        [
            pltpu.VMEM(tokens_shape, BF16),
            pltpu.VMEM((3, 2 * half, width), BF16),
            pltpu.VMEM((count, 2 * half), BF16),
            pltpu.VMEM((2 * heads * (positions // 8), block, block), F32),
            pltpu.VMEM((2 * half, count), F32),
            dma((7,)),
        ],
        flops=12 * count * half * width,
        nbytes=10_000_000,
        mib=63.1,
    )(moved, temporal_in, temporal_in_other)
    returned = lax.all_to_all(attended, "seq", 0, 0, tiled=True)
    tiles = width // LANES
    out = call(
        final_kernel,
        shape((count * tiles, LANES), F32),
        [HBM] * 4 + [VMEM],
        [
            pltpu.VMEM(tokens_shape, BF16),
            pltpu.VMEM((2 * half, width), BF16),
            pltpu.VMEM((count, width), F32),
            pltpu.VMEM((count * tiles, LANES), F32),
            dma((4 + CHUNKS,)),
        ],
        flops=4 * count * half * width,
        nbytes=8_000_000,
        out_specs=HBM,
        mib=63.1,
    )(returned, temporal_out, temporal_out_other, middle, temporal_mods)
    return out.reshape(frames.shape)


def solution(mesh):
    return jax.shard_map(
        body,
        mesh=mesh,
        in_specs=(
            P("tp", ("clip", "seq"), None),
            P("clip"),
            P(),
            P(("seq", "tp"), None),
            P(),
            P(),
            P(None, None, "tp"),
            P("tp", None),
            P(None, None, "tp"),
            P("tp", None),
        ),
        out_specs=P("tp", ("clip", "seq"), None),
        check_vma=False,
    )
```
